32 devices in a mesh: rows: 16 (over z, x, core), cols: 2 (over y).
Axes of the slice: x: 2, y: 2, z: 4, core: 2. Of those that a mesh axis runs over, the one named last changes fastest.
Arguments:
- matrix_blocks: bfloat16 [1024, 64, 1728], P(('rows', 'cols')), may hold values from -0.75 to 0.75
- restrict: bfloat16 [1024, 4096], P(('rows', 'cols')), may hold values from -1.5 to 1.5
- columns: int32 [1024, 27], P(('rows', 'cols')), may hold values from 0 to 191
- counts: int32 [1024], P(('rows', 'cols')), may hold values from 8 to 27, as said below
- aggregate: int32 [1024], P(('rows', 'cols')), may hold values from 0 to 1
Outputs:
- coarse: float32 [64, 64, 768], P(('rows', 'cols'))
The draws below stay inside these ranges and needn't reach their ends.
Inputs may be any that keep to these rules, and one draw needn't show every extreme that they name: `counts`: used slots are the first ones of a row; some row uses all 27.
All inputs are finite; a program needn't handle non-finite values.
Results may differ from the reference program's by a relative error of at most 0.0029.
Values may be sent and summed in bfloat16 or wider, within the bound.
No kernel may reach another device: no remote copies, remote signals or barrier semaphores. Data moves between devices by JAX's collectives and lax.ppermute only.
A program may use at most 192 MiB of HBM per device.

```python
import jax
import jax.numpy as jnp
from jax import lax

BLK = 64
SLOTS = 27
ROWS_DEV = 32
AGG_DEV = 2
SLAB = 64
WINDOW = 12
FINE = 1024
COARSE = 64
N_COLS = 2


def draw_counts(key, part):
    cap_key, row_key = jax.random.split(jax.random.fold_in(key, 11))
    blocks = FINE // ROWS_DEV
    caps = jax.random.randint(cap_key, (blocks,), 14, SLOTS + 1)
    caps = caps.at[0].set(SLOTS)
    per_row = jnp.repeat(caps, ROWS_DEV)
    raw_bits = jax.random.randint(row_key, (FINE,), 0, 1 << 20)
    row_counts = 8 + raw_bits % (per_row - 7)
    row_counts = row_counts.at[0].set(SLOTS)
    return row_counts.astype(jnp.int32)


def set_ends(drawn, stream_key, smallest, high):
    extent = drawn.shape
    spot = [jax.random.randint(jax.random.fold_in(stream_key, axis), (), 0, extent[axis]) for axis in range(len(extent))]
    drawn = drawn.at[tuple(spot)].set(smallest)
    longest = extent.index(max(extent))
    spot[longest] = (spot[longest] + 1) % extent[longest]
    return drawn.at[tuple(spot)].set(high)


def level_of(stream_key, dims, cuts, smallest, largest):
    def one(position, shards_of):
        draws = jax.random.uniform(jax.random.fold_in(jax.random.fold_in(stream_key, 6), position), (shards_of,), jnp.float32, smallest / len(cuts), largest / len(cuts))
        return jnp.repeat(jnp.exp(draws), dims[position] // shards_of).reshape((-1,) + (1,) * (len(dims) - position - 1))

    gain = one(*cuts[0])
    for cut in cuts[1:]:
        gain = gain * one(*cut)
    return gain


def normal_values(key, extent, width, limit, cuts=(), kind=jnp.bfloat16):
    array = jax.random.normal(key, extent, jnp.float32) * width
    if len(cuts) > 0:
        array = level_of(key, extent, cuts, -0.22, 0.18) * array
    return jnp.clip(array, min=-limit, max=limit).astype(kind)


def setup_inputs(seed: int = 0) -> dict:
    key_list = jax.random.split(jax.random.key(seed), 6)
    return {
        "matrix_blocks": normal_values(key_list[0], (FINE, BLK, SLOTS * BLK), BLK ** -0.5, 0.75, ((0, 32),)),
        "restrict": normal_values(key_list[1], (FINE, BLK * BLK), 0.25, 1.5, ((0, 32),)),
        "columns": set_ends(jax.random.randint(key_list[2], (FINE, SLOTS), 0, 3 * SLAB), jax.random.fold_in(key_list[2], 1), 0, (3 * SLAB) - 1).astype(jnp.int32),
        "counts": draw_counts(jax.random.fold_in(key_list[5], 71), 0),
        "aggregate": set_ends(jax.random.randint(key_list[4], (FINE,), 0, AGG_DEV), jax.random.fold_in(key_list[4], 1), 0, AGG_DEV - 1).astype(jnp.int32),
    }


def reference(matrix_blocks, restrict, columns, counts, aggregate):
    blocks = FINE // ROWS_DEV

    def one_device(device):
        first_row = device * ROWS_DEV
        a_rows = lax.dynamic_slice_in_dim(matrix_blocks, first_row, ROWS_DEV, 0)
        r_rows = lax.dynamic_slice_in_dim(restrict, first_row, ROWS_DEV, 0).reshape(ROWS_DEV, BLK, BLK)
        row_cols = lax.dynamic_slice_in_dim(columns, first_row, ROWS_DEV, 0)
        row_counts = lax.dynamic_slice_in_dim(counts, first_row, ROWS_DEV, 0)
        row_agg = lax.dynamic_slice_in_dim(aggregate, first_row, ROWS_DEV, 0)
        slab_index = device // N_COLS
        global_row = (slab_index - 1) * SLAB + row_cols
        slot_index = jnp.arange(SLOTS, dtype=jnp.int32)
        live_mask = (slot_index[None, :] < row_counts[:, None]) & (global_row >= 0) & (global_row < FINE)
        safe_row = jnp.clip(global_row, 0, FINE - 1).astype(jnp.int32)
        left_prod = jnp.einsum("ips,isn->ipn", r_rows.astype(jnp.float32), a_rows.astype(jnp.float32))
        left_prod = left_prod.astype(jnp.bfloat16).reshape(ROWS_DEV, BLK, SLOTS, BLK)
        far_blocks = restrict[safe_row.reshape(-1)].reshape(ROWS_DEV, SLOTS, BLK, BLK)
        products = jnp.einsum("ipks,ikqs->ikpq", left_prod.astype(jnp.float32), far_blocks.astype(jnp.float32))
        products = products * live_mask.astype(jnp.float32)[:, :, None, None]
        slot_ids = (row_cols // ROWS_DEV) * AGG_DEV + aggregate[safe_row]
        segment = row_agg[:, None] * WINDOW + slot_ids
        summed = jax.ops.segment_sum(products.reshape(ROWS_DEV * SLOTS, BLK, BLK), segment.reshape(-1).astype(jnp.int32), num_segments=AGG_DEV * WINDOW)
        return summed.reshape(AGG_DEV, WINDOW, BLK, BLK).transpose(0, 2, 1, 3).reshape(AGG_DEV, BLK, WINDOW * BLK)

    blocks_out = lax.map(one_device, jnp.arange(blocks, dtype=jnp.int32))
    return blocks_out.reshape(COARSE, BLK, WINDOW * BLK)
```

```python
import functools

import jax
import jax.numpy as jnp
from jax import lax
from jax.experimental import pallas as pl
from jax.experimental.pallas import tpu as pltpu
from jax.sharding import PartitionSpec as P

BLK = 64
SLOTS = 27
ROWS_DEV = 32
AGG_DEV = 2

LANES = 2 * BLK
PAIRS = ROWS_DEV // 2
HALF = PAIRS // 2
TAG = 16
HALF_ROWS = HALF * BLK + TAG
PAYLOAD = 2 * HALF_ROWS
ROW_PAIRS_STEP = 4
CHUNK = 6
MIB = 1 << 20


def pack_kernel(aggregate_ref, restrict_ref, out_ref, wide_ref):
    low = lax.broadcasted_iota(jnp.int32, (PAIRS, LANES), 1) < BLK
    for t in range(BLK // 2):
        x = restrict_ref[:, t * LANES : (t + 1) * LANES].astype(jnp.float32)
        first, second = x[:PAIRS], x[PAIRS:]
        even = jnp.where(low, first, pltpu.roll(second, BLK, 1))
        odd = jnp.where(low, pltpu.roll(first, BLK, 1), second)
        wide_ref[pl.ds(2 * t, PAIRS, stride=BLK), :] = even
        wide_ref[pl.ds(2 * t + 1, PAIRS, stride=BLK), :] = odd
    row = lax.broadcasted_iota(jnp.int32, (TAG, LANES), 0)
    low = lax.broadcasted_iota(jnp.int32, (TAG, LANES), 1) < BLK
    for half in range(2):
        base = half * HALF_ROWS
        out_ref[base : base + HALF * BLK, :] = wide_ref[
            half * HALF * BLK : (half + 1) * HALF * BLK, :
        ].astype(jnp.bfloat16)
        tags = jnp.zeros((TAG, LANES), jnp.int32)
        for p in range(HALF):
            g = half * HALF + p
            tags = jnp.where(
                row == p, jnp.where(low, aggregate_ref[g], aggregate_ref[g + PAIRS]), tags
            )
        out_ref[base + HALF * BLK : base + HALF_ROWS, :] = tags.astype(jnp.float32).astype(
            jnp.bfloat16
        )


def pack(aggregate, restrict):
    return pl.pallas_call(
        pack_kernel,
        out_shape=jax.ShapeDtypeStruct((PAYLOAD, LANES), jnp.bfloat16),
        in_specs=[
            pl.BlockSpec(memory_space=pltpu.SMEM),
            pl.BlockSpec(memory_space=pltpu.VMEM),
        ],
        out_specs=pl.BlockSpec(memory_space=pltpu.VMEM),
        scratch_shapes=[pltpu.VMEM((PAIRS * BLK, LANES), jnp.float32)],
        compiler_params=pltpu.CompilerParams(vmem_limit_bytes=8 * MIB),
        name="pack_payload",
    )(aggregate, restrict)


def left_kernel(order, columns_ref, counts_ref, aggregate_ref, payload_ref, matrix_ref, out_ref, sums_ref):
    chunk, step = pl.program_id(0), pl.program_id(1)
    steps = pl.num_programs(1)
    blocks = out_ref.shape[0]
    width = blocks * ROWS_DEV
    places = order()

    @pl.when(step == 0)
    def _():
        sums_ref[...] = jnp.zeros_like(sums_ref)

    lanes = lax.broadcasted_iota(jnp.int32, (BLK, LANES), 1)
    low, high = lanes < BLK, lanes >= BLK
    base = chunk * width

    def row_pair(local):
        pair = step * ROW_PAIRS_STEP + local
        half = pair // HALF
        start = pl.multiple_of(half * HALF_ROWS + (pair - half * HALF) * BLK, 16)
        both = payload_ref[pl.ds(start, BLK), :]
        zero = jnp.zeros_like(both)
        lhs = jnp.concatenate([jnp.where(low, both, zero), jnp.where(high, both, zero)], axis=0)
        rows = (pair, pair + PAIRS)
        places_of = []
        for row in rows:
            count = counts_ref[row]
            offset = aggregate_ref[row] * width
            places_of.append(
                [
                    jnp.where(
                        (k < count)
                        & (columns_ref[row, k] >= base)
                        & (columns_ref[row, k] < base + width),
                        offset + columns_ref[row, k] - base,
                        AGG_DEV * width,
                    )
                    for k in range(SLOTS)
                ]
            )
        for first in range(0, SLOTS, 4):
            many = min(4, SLOTS - first)
            cut = slice(first * BLK, (first + many) * BLK)
            rhs = jnp.concatenate(
                [matrix_ref[0, local, :, cut], matrix_ref[1, local, :, cut]], axis=0
            )
            left = jnp.dot(lhs, rhs, preferred_element_type=jnp.float32)
            left = left.astype(jnp.bfloat16).astype(jnp.float32)
            for r in range(2):
                for k in range(0, many, 2):
                    x = left[r * BLK : (r + 1) * BLK, k * BLK : min(k + 2, many) * BLK]
                    place = places_of[r][first + k]
                    if k + 1 < many:
                        other = places_of[r][first + k + 1]
                        x_low = sums_ref[place] + x
                        x_high = sums_ref[other] + x
                        pltpu.store(sums_ref.at[place], x_low, mask=low)
                        pltpu.store(sums_ref.at[other], x_high, mask=high)
                    else:
                        sums_ref[place, :, :BLK] = sums_ref[place, :, :BLK] + x

    for local in range(ROW_PAIRS_STEP):
        row_pair(local)

    @pl.when(step == steps - 1)
    def _():
        for position in range(blocks):
            start = (places[position] if places is not None else position) * ROWS_DEV
            for a in range(AGG_DEV):
                for p in range(PAIRS):
                    g = a * width + start + p
                    one, two = sums_ref[g], sums_ref[g + PAIRS]
                    one = one + pltpu.roll(one, BLK, 1)
                    two = two + pltpu.roll(two, BLK, 1)
                    out_ref[position, a * BLK : (a + 1) * BLK, p * LANES : (p + 1) * LANES] = (
                        jnp.where(low, one, two).astype(jnp.bfloat16)
                    )


def left_sums(columns, counts, aggregate, payload, matrix_blocks, total, order):
    blocks = CHUNK if total % CHUNK == 0 else CHUNK // 2
    matrix = matrix_blocks.reshape(2, PAIRS, BLK, SLOTS * BLK)
    steps = PAIRS // ROW_PAIRS_STEP
    smem = pl.BlockSpec(memory_space=pltpu.SMEM)
    return pl.pallas_call(
        functools.partial(left_kernel, order),
        grid=(total // blocks, steps),
        out_shape=jax.ShapeDtypeStruct((total, AGG_DEV * BLK, PAIRS * LANES), jnp.bfloat16),
        in_specs=[
            smem,
            smem,
            smem,
            pl.BlockSpec((PAYLOAD, LANES), lambda c, s: (0, 0)),
            pl.BlockSpec((2, ROW_PAIRS_STEP, BLK, SLOTS * BLK), lambda c, s: (0, s, 0, 0)),
        ],
        out_specs=pl.BlockSpec((blocks, AGG_DEV * BLK, PAIRS * LANES), lambda c, s: (c, 0, 0)),
        scratch_shapes=[
            pltpu.VMEM((AGG_DEV * blocks * ROWS_DEV + 1, BLK, LANES), jnp.float32)
        ],
        compiler_params=pltpu.CompilerParams(vmem_limit_bytes=40 * MIB),
        cost_estimate=pl.CostEstimate(
            flops=2 * ROWS_DEV * SLOTS * BLK**3, bytes_accessed=12 * MIB, transcendentals=0
        ),
        name="left_sums",
    )(columns, counts, aggregate, payload, matrix)


def half_product(lefts, half, piece):
    tags = piece[HALF * BLK : HALF_ROWS, :].astype(jnp.float32)
    masks = [(tags == j).astype(jnp.float32).astype(jnp.bfloat16) for j in range(AGG_DEV)]
    rhs = jnp.concatenate(
        [
            jnp.concatenate(
                [piece[p * BLK : (p + 1) * BLK, :] * masks[j][p : p + 1, :] for p in range(HALF)],
                axis=1,
            )
            for j in range(AGG_DEV)
        ],
        axis=0,
    )
    cut = lefts[:, half * HALF * LANES : (half + 1) * HALF * LANES]
    return lax.dot_general(
        cut, rhs, (((1,), (1,)), ((), ())), preferred_element_type=jnp.float32
    )


def right_kernel(sources, order, first, carried, lefts_ref, *refs):
    out_ref = refs[-1]
    if carried:
        out_ref[...] = refs[-2][...]
    places = order()
    for position, halves in enumerate(sources):
        lefts = lefts_ref[position]
        total = 0.0
        for half, (index, start) in enumerate(halves):
            piece = refs[index][start : start + HALF_ROWS, :]
            total = total + half_product(lefts, half, piece)
        place = places[first + position]
        if not isinstance(place, int):
            place = pl.multiple_of(place * LANES, LANES)
        else:
            place = place * LANES
        for a in range(AGG_DEV):
            out_ref[a, :, pl.ds(place, LANES)] = total[a * BLK : (a + 1) * BLK]


def right_products(lefts, pieces, sources, order, first, width, so_far):
    carried = so_far is not None
    many = len(sources)
    vmem = pl.BlockSpec(memory_space=pltpu.VMEM)
    shape = jax.ShapeDtypeStruct((AGG_DEV, BLK, width), jnp.float32)
    return pl.pallas_call(
        functools.partial(right_kernel, sources, order, first, carried),
        grid=(1,),
        out_shape=shape,
        in_specs=[
            pl.BlockSpec((many,) + lefts.shape[1:], lambda s: (first // many, 0, 0))
        ]
        + [pl.BlockSpec(piece.shape, lambda s: (0, 0)) for piece in pieces]
        + ([pl.BlockSpec(shape.shape, lambda s: (0, 0, 0))] if carried else []),
        out_specs=pl.BlockSpec(shape.shape, lambda s: (0, 0, 0)),
        compiler_params=pltpu.CompilerParams(vmem_limit_bytes=24 * MIB),
        cost_estimate=pl.CostEstimate(
            flops=2 * many * (AGG_DEV * BLK) ** 2 * PAIRS * LANES,
            bytes_accessed=many * 2 * MIB,
            transcendentals=0,
        ),
        name="right_products",
    )(lefts, *pieces, *([so_far] if carried else []))


def paired_plan(columns, counts, aggregate, matrix_blocks, payload, row_count):
    odds = [(i, i + 1) for i in range(1, row_count - 1, 2)]
    odds = odds + [(b, a) for a, b in odds]
    evens = [(i, i ^ 1) for i in range(row_count)]
    across = lambda x: lax.ppermute(x, "cols", [(0, 1), (1, 0)])
    even = lambda x: lax.ppermute(x, "rows", evens)
    odd = lambda x: lax.ppermute(x, "rows", odds)

    def order():
        c, up = lax.axis_index("cols"), 1 - lax.rem(lax.axis_index("rows"), 2)
        near, far = 4 * up, 4 * (1 - up)
        return [2 + c, 3 - c, near + c, near + 1 - c, far + c, far + 1 - c]

    beside = across(payload)
    ahead = odd(payload)
    inner = even(payload)
    inner_beside = even(beside)
    far_first = odd(beside[:HALF_ROWS])
    far_second = across(ahead[HALF_ROWS:])
    lefts = left_sums(columns, counts, aggregate, payload, matrix_blocks, 6, order)
    whole = lambda index: ((index, 0), (index, HALF_ROWS))
    near = right_products(
        lefts,
        [payload, beside, inner, inner_beside],
        [whole(0), whole(1), whole(2), whole(3)],
        order,
        0,
        6 * LANES,
        None,
    )
    return right_products(
        lefts,
        [ahead, far_first, far_second],
        [whole(0), ((1, 0), (2, 0))],
        order,
        4,
        6 * LANES,
        near,
    )


def general_plan(columns, counts, aggregate, matrix_blocks, payload, row_count, col_count):
    forward = [(i, i + 1) for i in range(row_count - 1)]
    backward = [(b, a) for a, b in forward]
    slab = lax.all_gather(payload, "cols", axis=0, tiled=True)
    pieces = [lax.ppermute(slab, "rows", forward), slab, lax.ppermute(slab, "rows", backward)]
    total = 3 * col_count
    order = lambda: list(range(total))
    lefts = left_sums(columns, counts, aggregate, payload, matrix_blocks, total, lambda: None)
    sources = [
        tuple((s, (c * 2 + half) * HALF_ROWS) for half in range(2))
        for s in range(3)
        for c in range(col_count)
    ]
    return right_products(lefts, pieces, sources, order, 0, total * LANES, None)


def per_device(matrix_blocks, restrict, columns, counts, aggregate):
    col_count = lax.axis_size("cols")
    row_count = lax.axis_size("rows")
    payload = pack(aggregate, restrict)
    if col_count == 2 and row_count % 2 == 0:
        return paired_plan(columns, counts, aggregate, matrix_blocks, payload, row_count)
    return general_plan(
        columns, counts, aggregate, matrix_blocks, payload, row_count, col_count
    )


def solution(mesh):
    return jax.shard_map(
        per_device,
        mesh=mesh,
        in_specs=(
            P(("rows", "cols"), None, None),
            P(("rows", "cols"), None),
            P(("rows", "cols"), None),
            P(("rows", "cols")),
            P(("rows", "cols")),
        ),
        out_specs=P(("rows", "cols"), None, None),
        check_vma=False,
    )
```

```python
import functools

import jax
import jax.numpy as jnp
from jax import lax
from jax.experimental import pallas as pl
from jax.experimental.pallas import tpu as pltpu
from jax.sharding import PartitionSpec as P

BLK = 64
SLOTS = 27
ROWS_DEV = 32
AGG_DEV = 2

LANES = 2 * BLK
PAIRS = ROWS_DEV // 2
HALF = PAIRS // 2
TAG = 16
HALF_ROWS = HALF * BLK + TAG
PAYLOAD = 2 * HALF_ROWS
STEP = 4
DEPTH = 2
CHUNK = 6
MIB = 1 << 20


def pack_kernel(aggregate_hbm, restrict_hbm, out_ref, restrict_ref, wide_ref, aggregate_ref, sems):
    rows = pltpu.make_async_copy(restrict_hbm, restrict_ref, sems.at[0])
    tags = pltpu.make_async_copy(aggregate_hbm, aggregate_ref, sems.at[1])
    rows.start()
    tags.start()
    tags.wait()
    row = lax.broadcasted_iota(jnp.int32, (TAG, LANES), 0)
    low = lax.broadcasted_iota(jnp.int32, (TAG, LANES), 1) < BLK
    for half in range(2):
        owners = jnp.zeros((TAG, LANES), jnp.int32)
        for p in range(HALF):
            g = half * HALF + p
            owners = jnp.where(
                row == p, jnp.where(low, aggregate_ref[g], aggregate_ref[g + PAIRS]), owners
            )
        last = (half + 1) * HALF_ROWS
        out_ref[last - TAG : last, :] = owners.astype(jnp.float32).astype(jnp.bfloat16)
    rows.wait()
    low = lax.broadcasted_iota(jnp.int32, (PAIRS, LANES), 1) < BLK
    for t in range(BLK // 2):
        x = restrict_ref[:, t * LANES : (t + 1) * LANES].astype(jnp.float32)
        first, second = x[:PAIRS], x[PAIRS:]
        even = jnp.where(low, first, pltpu.roll(second, BLK, 1))
        odd = jnp.where(low, pltpu.roll(first, BLK, 1), second)
        wide_ref[pl.ds(2 * t, PAIRS, stride=BLK), :] = even
        wide_ref[pl.ds(2 * t + 1, PAIRS, stride=BLK), :] = odd
    for half in range(2):
        out_ref[half * HALF_ROWS : half * HALF_ROWS + HALF * BLK, :] = wide_ref[
            half * HALF * BLK : (half + 1) * HALF * BLK, :
        ].astype(jnp.bfloat16)


def pack(aggregate, restrict):
    hbm = pl.BlockSpec(memory_space=pltpu.HBM)
    return pl.pallas_call(
        pack_kernel,
        out_shape=jax.ShapeDtypeStruct((PAYLOAD, LANES), jnp.bfloat16),
        in_specs=[hbm, hbm],
        out_specs=pl.BlockSpec(memory_space=pltpu.VMEM),
        scratch_shapes=[
            pltpu.VMEM(restrict.shape, restrict.dtype),
            pltpu.VMEM((PAIRS * BLK, LANES), jnp.float32),
            pltpu.SMEM(aggregate.shape, aggregate.dtype),
            pltpu.SemaphoreType.DMA((2,)),
        ],
        compiler_params=pltpu.CompilerParams(vmem_limit_bytes=8 * MIB),
        name="pack_payload",
    )(*(pltpu.with_memory_space_constraint(x, pltpu.HBM) for x in (aggregate, restrict)))


def left_kernel(
    order,
    columns_hbm,
    counts_hbm,
    aggregate_hbm,
    payload_ref,
    matrix_hbm,
    out_ref,
    matrix_ref,
    sums_ref,
    columns_ref,
    counts_ref,
    aggregate_ref,
    matrix_sems,
    sems,
):
    total = out_ref.shape[0]
    blocks = CHUNK if total % CHUNK == 0 else CHUNK // 2
    width = blocks * ROWS_DEV
    places = order()
    short = BLK // 2
    steps = PAIRS // STEP

    def rows_copy(step):
        cut = pl.ds(step * STEP, STEP)
        return pltpu.make_async_copy(
            matrix_hbm.at[:, cut], matrix_ref.at[:, cut], matrix_sems.at[step]
        )

    small = [
        pltpu.make_async_copy(columns_hbm, columns_ref, sems.at[0]),
        pltpu.make_async_copy(counts_hbm, counts_ref, sems.at[1]),
        pltpu.make_async_copy(aggregate_hbm, aggregate_ref, sems.at[2]),
    ]
    for copy in small:
        copy.start()
    for step in range(steps):
        rows_copy(step).start()
    low = lax.broadcasted_iota(jnp.int32, (BLK, LANES), 1) < BLK
    low_short = lax.broadcasted_iota(jnp.int32, (short, LANES), 1) < BLK

    def add_all(entries):
        waiting = []
        for place, tile in entries:
            value = sums_ref[place]
            for earlier, earlier_value in waiting:
                value = jnp.where(place == earlier, earlier_value, value)
            value = value + tile
            if len(waiting) == DEPTH:
                sums_ref[waiting[0][0]] = waiting[0][1]
                waiting = waiting[1:]
            waiting = waiting + [(place, value)]
        for place, value in waiting:
            sums_ref[place] = value

    def tiles_of(base, pair):
        half = pair // HALF
        start = pl.multiple_of(half * HALF_ROWS + (pair - half * HALF) * BLK, 16)
        both = payload_ref[pl.ds(start, BLK), :]
        zero = jnp.zeros_like(both)
        lhs = jnp.concatenate([jnp.where(low, both, zero), jnp.where(low, zero, both)], axis=0)
        rows = (pair, pair + PAIRS)
        count = [counts_ref[row] for row in rows]
        offset = [aggregate_ref[row] * width for row in rows]

        def place_of(r, k):
            local = columns_ref[rows[r], k]
            live = k < count[r]
            if total > blocks:
                local = local - base
                live = live & (local >= 0) & (local < width)
            return jnp.where(live, offset[r] + local, AGG_DEV * width)

        for first in range(0, SLOTS, 4):
            many = min(4, SLOTS - first)
            cut = slice(first * BLK, (first + many) * BLK)
            rhs = jnp.concatenate(
                [matrix_ref[0, pair, :, cut], matrix_ref[1, pair, :, cut]], axis=0
            )
            if many * BLK % LANES:
                rhs = jnp.concatenate([rhs, rhs[:, -BLK:]], axis=1)
            left = jnp.dot(lhs, rhs, preferred_element_type=jnp.float32).astype(jnp.bfloat16)
            for k in range(0, many, 2):
                for r in range(2):
                    lanes = slice(k * BLK, (k + 2) * BLK)
                    upper = left[r * BLK : r * BLK + short, lanes]
                    lower = left[r * BLK + short : (r + 1) * BLK, lanes]
                    one = jnp.where(low_short, upper, pltpu.roll(lower, BLK, 1))
                    yield place_of(r, first + k), one.astype(jnp.float32)
                    if k + 1 < many:
                        two = jnp.where(low_short, pltpu.roll(upper, BLK, 1), lower)
                        yield place_of(r, first + k + 1), two.astype(jnp.float32)

    def one_chunk(chunk, first_chunk):
        base = chunk * width
        sums_ref[...] = jnp.zeros_like(sums_ref)
        if first_chunk:
            for copy in small:
                copy.wait()

        def one_step(step, carry):
            if first_chunk:
                rows_copy(step).wait()
            add_all(
                entry for local in range(STEP) for entry in tiles_of(base, step * STEP + local)
            )
            return carry

        lax.fori_loop(0, steps, one_step, 0)
        for position in range(blocks):
            spot, live = places[position] if places is not None else (position, None)
            start = spot * ROWS_DEV
            for a in range(AGG_DEV):
                for p in range(PAIRS):
                    g = a * width + start + p
                    one, two = sums_ref[g], sums_ref[g + PAIRS]
                    if live is not None:
                        one, two = jnp.where(live, one, 0.0), jnp.where(live, two, 0.0)
                    one, two = one.astype(jnp.bfloat16), two.astype(jnp.bfloat16)
                    lanes = slice(p * LANES, (p + 1) * LANES)
                    out_ref[chunk * blocks + position, a * BLK : a * BLK + short, lanes] = (
                        jnp.where(low_short, one, pltpu.roll(two, BLK, 1))
                    )
                    out_ref[
                        chunk * blocks + position, a * BLK + short : (a + 1) * BLK, lanes
                    ] = jnp.where(low_short, pltpu.roll(one, BLK, 1), two)

    one_chunk(0, True)
    if total > blocks:

        def later(chunk, carry):
            one_chunk(chunk, False)
            return carry

        lax.fori_loop(1, total // blocks, later, 0)


def left_sums(columns, counts, aggregate, payload, matrix_blocks, total, order):
    blocks = CHUNK if total % CHUNK == 0 else CHUNK // 2
    matrix = matrix_blocks.reshape(2, PAIRS, BLK, SLOTS * BLK)
    hbm = pl.BlockSpec(memory_space=pltpu.HBM)
    vmem = pl.BlockSpec(memory_space=pltpu.VMEM)
    return pl.pallas_call(
        functools.partial(left_kernel, order),
        out_shape=jax.ShapeDtypeStruct((total, AGG_DEV * BLK, PAIRS * LANES), jnp.bfloat16),
        in_specs=[hbm, hbm, hbm, vmem, hbm],
        out_specs=vmem,
        scratch_shapes=[
            pltpu.VMEM(matrix.shape, matrix.dtype),
            pltpu.VMEM((AGG_DEV * blocks * ROWS_DEV + 1, BLK // 2, LANES), jnp.float32),
            pltpu.SMEM(columns.shape, columns.dtype),
            pltpu.SMEM(counts.shape, counts.dtype),
            pltpu.SMEM(aggregate.shape, aggregate.dtype),
            pltpu.SemaphoreType.DMA((PAIRS // STEP,)),
            pltpu.SemaphoreType.DMA((3,)),
        ],
        compiler_params=pltpu.CompilerParams(vmem_limit_bytes=20 * MIB),
        cost_estimate=pl.CostEstimate(
            flops=40 * ROWS_DEV * SLOTS * BLK**3, bytes_accessed=12 * MIB, transcendentals=0
        ),
        name="left_sums",
    )(
        *(pltpu.with_memory_space_constraint(x, pltpu.HBM) for x in (columns, counts, aggregate)),
        payload,
        pltpu.with_memory_space_constraint(matrix, pltpu.HBM),
    )


def half_product(lefts, half, piece):
    tags = piece[HALF * BLK : HALF_ROWS, :].astype(jnp.float32)
    masks = [(tags == j).astype(jnp.float32).astype(jnp.bfloat16) for j in range(AGG_DEV)]
    rhs = jnp.concatenate(
        [
            jnp.concatenate(
                [piece[p * BLK : (p + 1) * BLK, :] * masks[j][p : p + 1, :] for p in range(HALF)],
                axis=1,
            )
            for j in range(AGG_DEV)
        ],
        axis=0,
    )
    cut = lefts[:, half * HALF * LANES : (half + 1) * HALF * LANES]
    return lax.dot_general(
        cut, rhs, (((1,), (1,)), ((), ())), preferred_element_type=jnp.float32
    )


def right_kernel(sources, order, first, carried, lefts_ref, *refs):
    out_ref = refs[-1]
    if carried:
        out_ref[...] = refs[-2][...]
    places = order()
    for position, halves in enumerate(sources):
        lefts = lefts_ref[first + position]
        total = 0.0
        for half, (index, start) in enumerate(halves):
            piece = refs[index][start : start + HALF_ROWS, :]
            total = total + half_product(lefts, half, piece)
        place, _ = places[first + position]
        if not isinstance(place, int):
            place = pl.multiple_of(place * LANES, LANES)
        else:
            place = place * LANES
        for a in range(AGG_DEV):
            out_ref[a, :, pl.ds(place, LANES)] = total[a * BLK : (a + 1) * BLK]


def right_products(lefts, pieces, sources, order, first, width, so_far, last):
    carried = so_far is not None
    many = len(sources)
    vmem = pl.BlockSpec(memory_space=pltpu.VMEM)
    shape = jax.ShapeDtypeStruct((AGG_DEV, BLK, width), jnp.float32)
    return pl.pallas_call(
        functools.partial(right_kernel, sources, order, first, carried),
        grid=(1,),
        out_shape=shape,
        in_specs=[vmem] * (1 + len(pieces) + carried),
        out_specs=pl.BlockSpec(shape.shape, lambda s: (0, 0, 0)) if last else vmem,
        compiler_params=pltpu.CompilerParams(vmem_limit_bytes=8 * MIB),
        cost_estimate=pl.CostEstimate(
            flops=2 * many * (AGG_DEV * BLK) ** 2 * PAIRS * LANES,
            bytes_accessed=many * MIB // 16,
            transcendentals=0,
        ),
        name="right_products",
    )(lefts, *pieces, *([so_far] if carried else []))


def paired_plan(columns, counts, aggregate, matrix_blocks, payload, row_count):
    ring = [(i, (i + 1) % row_count) for i in range(row_count)]
    across = [(0, 1), (1, 0)]
    evens = [(i, i ^ 1) for i in range(row_count)]
    odds = [(i, i + 1) for i in range(1, row_count - 1, 2)]
    odds = odds + [(b, a) for a, b in odds] + [(0, 0), (row_count - 1, row_count - 1)]
    crossed = [(2 * a + c, 2 * b + 1 - c) for a, b in odds for c in range(2)]

    def order():
        c, row = lax.axis_index("cols"), lax.axis_index("rows")
        up = 1 - lax.rem(row, 2)
        inside = [row > 0, None, row < row_count - 1]
        spots = [(1, c), (1, 1 - c), (0, c), (2, c), (2 * up, 1 - c), (2 - 2 * up, 1 - c)]
        far = (up == 0) & (row < row_count - 1) | (up == 1) & (row > 0)
        return [(2 * slab + col, live) for (slab, col), live in zip(spots, [None, None, inside[0], inside[2], None, far])]

    far = lax.ppermute(payload, ("rows", "cols"), crossed)
    below = lax.ppermute(payload, "rows", ring)
    above = lax.ppermute(payload, "rows", [(b, a) for a, b in ring])
    beside = lax.ppermute(payload, "cols", across)
    lefts = left_sums(columns, counts, aggregate, payload, matrix_blocks, 6, order)
    lefts, beside = lax.optimization_barrier((lefts, beside))
    inner = lax.ppermute(beside, "rows", evens)
    whole = lambda index: ((index, 0), (index, HALF_ROWS))
    return right_products(
        lefts,
        [payload, beside, below, above, inner, far],
        [whole(index) for index in range(6)],
        order,
        0,
        6 * LANES,
        None,
        True,
    )


def general_plan(columns, counts, aggregate, matrix_blocks, payload, row_count, col_count):
    forward = [(i, i + 1) for i in range(row_count - 1)]
    backward = [(b, a) for a, b in forward]
    slab = lax.all_gather(payload, "cols", axis=0, tiled=True)
    pieces = [lax.ppermute(slab, "rows", forward), slab, lax.ppermute(slab, "rows", backward)]
    total = 3 * col_count
    order = lambda: [(block, None) for block in range(total)]
    lefts = left_sums(columns, counts, aggregate, payload, matrix_blocks, total, lambda: None)
    sources = [
        tuple((s, (c * 2 + half) * HALF_ROWS) for half in range(2))
        for s in range(3)
        for c in range(col_count)
    ]
    return right_products(lefts, pieces, sources, order, 0, total * LANES, None, True)


def per_device(matrix_blocks, restrict, columns, counts, aggregate):
    col_count = lax.axis_size("cols")
    row_count = lax.axis_size("rows")
    payload = pack(aggregate, restrict)
    if col_count == 2 and row_count % 2 == 0:
        return paired_plan(columns, counts, aggregate, matrix_blocks, payload, row_count)
    return general_plan(
        columns, counts, aggregate, matrix_blocks, payload, row_count, col_count
    )


def solution(mesh):
    return jax.shard_map(
        per_device,
        mesh=mesh,
        in_specs=(
            P(("rows", "cols"), None, None),
            P(("rows", "cols"), None),
            P(("rows", "cols"), None),
            P(("rows", "cols")),
            P(("rows", "cols")),
        ),
        out_specs=P(("rows", "cols"), None, None),
        check_vma=False,
    )
```

```python
import functools

import jax
import jax.numpy as jnp
from jax import lax
from jax.experimental import pallas as pl
from jax.experimental.pallas import tpu as pltpu
from jax.sharding import PartitionSpec as P

BLK = 64
SLOTS = 27
ROWS_DEV = 32
AGG_DEV = 2

LANES = 2 * BLK
PAIRS = ROWS_DEV // 2
TAGS = PAIRS * BLK
PAYLOAD = TAGS + PAIRS
STEP = 4
BATCH = 4
CHUNK = 6
MIB = 1 << 20


def pack_kernel(aggregate_hbm, restrict_hbm, out_ref, restrict_ref, wide_ref, aggregate_ref, sems):
    rows = pltpu.make_async_copy(restrict_hbm, restrict_ref, sems.at[0])
    tags = pltpu.make_async_copy(aggregate_hbm, aggregate_ref, sems.at[1])
    rows.start()
    tags.start()
    tags.wait()
    row = lax.broadcasted_iota(jnp.int32, (PAIRS, LANES), 0)
    low = lax.broadcasted_iota(jnp.int32, (PAIRS, LANES), 1) < BLK
    owners = jnp.zeros((PAIRS, LANES), jnp.int32)
    for p in range(PAIRS):
        owner = jnp.where(low, aggregate_ref[p], aggregate_ref[p + PAIRS])
        owners = jnp.where(row == p, owner, owners)
    out_ref[TAGS:, :] = owners.astype(jnp.float32).astype(jnp.bfloat16)
    rows.wait()
    for t in range(BLK // 2):
        x = restrict_ref[:, t * LANES : (t + 1) * LANES].astype(jnp.float32)
        first, second = x[:PAIRS], x[PAIRS:]
        even = jnp.where(low, first, pltpu.roll(second, BLK, 1))
        odd = jnp.where(low, pltpu.roll(first, BLK, 1), second)
        wide_ref[pl.ds(2 * t, PAIRS, stride=BLK), :] = even
        wide_ref[pl.ds(2 * t + 1, PAIRS, stride=BLK), :] = odd
    out_ref[:TAGS, :] = wide_ref[...].astype(jnp.bfloat16)


def pack(aggregate, restrict):
    hbm = pl.BlockSpec(memory_space=pltpu.HBM)
    return pl.pallas_call(
        pack_kernel,
        out_shape=jax.ShapeDtypeStruct((PAYLOAD, LANES), jnp.bfloat16),
        in_specs=[hbm, hbm],
        out_specs=pl.BlockSpec(memory_space=pltpu.VMEM),
        scratch_shapes=[
            pltpu.VMEM(restrict.shape, restrict.dtype),
            pltpu.VMEM((PAIRS * BLK, LANES), jnp.float32),
            pltpu.SMEM(aggregate.shape, aggregate.dtype),
            pltpu.SemaphoreType.DMA((2,)),
        ],
        compiler_params=pltpu.CompilerParams(vmem_limit_bytes=8 * MIB),
        name="pack_payload",
    )(*(pltpu.with_memory_space_constraint(x, pltpu.HBM) for x in (aggregate, restrict)))


def left_kernel(
    order,
    columns_hbm,
    counts_hbm,
    aggregate_hbm,
    payload_ref,
    matrix_hbm,
    out_ref,
    matrix_ref,
    sums_ref,
    columns_ref,
    counts_ref,
    aggregate_ref,
    matrix_sems,
    sems,
):
    total = out_ref.shape[0]
    blocks = CHUNK if total % CHUNK == 0 else CHUNK // 2
    width = blocks * ROWS_DEV
    places = order()
    short = BLK // 2
    steps = PAIRS // STEP

    def rows_copy(step):
        cut = pl.ds(step * STEP, STEP)
        return pltpu.make_async_copy(
            matrix_hbm.at[:, cut], matrix_ref.at[:, cut], matrix_sems.at[step]
        )

    small = [
        pltpu.make_async_copy(columns_hbm, columns_ref, sems.at[0]),
        pltpu.make_async_copy(counts_hbm, counts_ref, sems.at[1]),
        pltpu.make_async_copy(aggregate_hbm, aggregate_ref, sems.at[2]),
    ]
    for copy in small:
        copy.start()
    for step in range(steps):
        rows_copy(step).start()
    low = lax.broadcasted_iota(jnp.int32, (BLK, LANES), 1) < BLK
    low_short = lax.broadcasted_iota(jnp.int32, (short, LANES), 1) < BLK

    def add_all(entries):
        entries = list(entries)
        for first in range(0, len(entries), BATCH):
            batch = entries[first : first + BATCH]
            values = [sums_ref[place] for place, _ in batch]
            for n, (place, tile) in enumerate(batch):
                for earlier in range(n):
                    values[n] = jnp.where(place == batch[earlier][0], values[earlier], values[n])
                values[n] = values[n] + tile
            for (place, _), value in zip(batch, values):
                sums_ref[place] = value

    def tiles_of(base, pair):
        both = payload_ref[pl.ds(pl.multiple_of(pair * BLK, BLK), BLK), :]
        zero = jnp.zeros_like(both)
        lhs = jnp.concatenate([jnp.where(low, both, zero), jnp.where(low, zero, both)], axis=0)
        rows = (pair, pair + PAIRS)
        count = [counts_ref[row] for row in rows]
        offset = [aggregate_ref[row] * width for row in rows]

        def place_of(r, k):
            local = columns_ref[rows[r], k]
            live = k < count[r]
            if total > blocks:
                local = local - base
                live = live & (local >= 0) & (local < width)
            return jnp.where(live, offset[r] + local, AGG_DEV * width)

        for first in range(0, SLOTS, 4):
            many = min(4, SLOTS - first)
            cut = slice(first * BLK, (first + many) * BLK)
            rhs = jnp.concatenate(
                [matrix_ref[0, pair, :, cut], matrix_ref[1, pair, :, cut]], axis=0
            )
            if many * BLK % LANES:
                rhs = jnp.concatenate([rhs, rhs[:, -BLK:]], axis=1)
            left = jnp.dot(lhs, rhs, preferred_element_type=jnp.float32).astype(jnp.bfloat16)
            for k in range(0, many, 2):
                for r in range(2):
                    lanes = slice(k * BLK, (k + 2) * BLK)
                    upper = left[r * BLK : r * BLK + short, lanes]
                    lower = left[r * BLK + short : (r + 1) * BLK, lanes]
                    one = jnp.where(low_short, upper, pltpu.roll(lower, BLK, 1))
                    yield place_of(r, first + k), one.astype(jnp.float32)
                    if k + 1 < many:
                        two = jnp.where(low_short, pltpu.roll(upper, BLK, 1), lower)
                        yield place_of(r, first + k + 1), two.astype(jnp.float32)

    def one_chunk(chunk, first_chunk):
        base = chunk * width
        sums_ref[...] = jnp.zeros_like(sums_ref)
        if first_chunk:
            for copy in small:
                copy.wait()

        def one_step(step, carry):
            if first_chunk:
                rows_copy(step).wait()
            add_all(
                entry for local in range(STEP) for entry in tiles_of(base, step * STEP + local)
            )
            return carry

        lax.fori_loop(0, steps, one_step, 0)
        for position in range(blocks):
            spot, live = places[position] if places is not None else (position, None)
            start = spot * ROWS_DEV
            for a in range(AGG_DEV):
                for p in range(PAIRS):
                    g = a * width + start + p
                    one, two = sums_ref[g], sums_ref[g + PAIRS]
                    if live is not None:
                        one, two = jnp.where(live, one, 0.0), jnp.where(live, two, 0.0)
                    one, two = one.astype(jnp.bfloat16), two.astype(jnp.bfloat16)
                    lanes = slice(p * LANES, (p + 1) * LANES)
                    out_ref[chunk * blocks + position, a * BLK : a * BLK + short, lanes] = (
                        jnp.where(low_short, one, pltpu.roll(two, BLK, 1))
                    )
                    out_ref[
                        chunk * blocks + position, a * BLK + short : (a + 1) * BLK, lanes
                    ] = jnp.where(low_short, pltpu.roll(one, BLK, 1), two)

    one_chunk(0, True)
    if total > blocks:

        def later(chunk, carry):
            one_chunk(chunk, False)
            return carry

        lax.fori_loop(1, total // blocks, later, 0)


def left_sums(columns, counts, aggregate, payload, matrix_blocks, total, order):
    blocks = CHUNK if total % CHUNK == 0 else CHUNK // 2
    matrix = matrix_blocks.reshape(2, PAIRS, BLK, SLOTS * BLK)
    hbm = pl.BlockSpec(memory_space=pltpu.HBM)
    vmem = pl.BlockSpec(memory_space=pltpu.VMEM)
    return pl.pallas_call(
        functools.partial(left_kernel, order),
        out_shape=jax.ShapeDtypeStruct((total, AGG_DEV * BLK, PAIRS * LANES), jnp.bfloat16),
        in_specs=[hbm, hbm, hbm, vmem, hbm],
        out_specs=vmem,
        scratch_shapes=[
            pltpu.VMEM(matrix.shape, matrix.dtype),
            pltpu.VMEM((AGG_DEV * blocks * ROWS_DEV + 1, BLK // 2, LANES), jnp.float32),
            pltpu.SMEM(columns.shape, columns.dtype),
            pltpu.SMEM(counts.shape, counts.dtype),
            pltpu.SMEM(aggregate.shape, aggregate.dtype),
            pltpu.SemaphoreType.DMA((PAIRS // STEP,)),
            pltpu.SemaphoreType.DMA((3,)),
        ],
        compiler_params=pltpu.CompilerParams(vmem_limit_bytes=20 * MIB),
        cost_estimate=pl.CostEstimate(
            flops=4 * ROWS_DEV * SLOTS * BLK**3, bytes_accessed=4 * MIB // 2, transcendentals=0
        ),
        name="left_sums",
    )(
        *(pltpu.with_memory_space_constraint(x, pltpu.HBM) for x in (columns, counts, aggregate)),
        payload,
        pltpu.with_memory_space_constraint(matrix, pltpu.HBM),
    )


def block_product(lefts, piece):
    tags = piece[TAGS:, :].astype(jnp.float32)
    masks = [(tags == j).astype(jnp.float32).astype(jnp.bfloat16) for j in range(AGG_DEV)]
    rhs = jnp.concatenate(
        [
            jnp.concatenate(
                [piece[p * BLK : (p + 1) * BLK, :] * masks[j][p : p + 1, :] for p in range(PAIRS)],
                axis=1,
            )
            for j in range(AGG_DEV)
        ],
        axis=0,
    )
    return lax.dot_general(
        lefts, rhs, (((1,), (1,)), ((), ())), preferred_element_type=jnp.float32
    )


def right_kernel(sources, order, first, carried, lefts_ref, *refs):
    refs = list(refs)
    before = refs.pop(-4) if carried else None
    out_hbm, columns_ref, sems = refs[-3:]
    copies = []
    for position, (index, start) in enumerate(sources):
        total = block_product(
            lefts_ref[first + position], refs[index][start : start + PAYLOAD, :]
        )
        place, _ = order()[first + position]
        place = place * LANES if isinstance(place, int) else pl.multiple_of(place * LANES, LANES)
        for a in range(AGG_DEV):
            columns_ref[position, a] = total[a * BLK : (a + 1) * BLK]
        copy = pltpu.make_async_copy(
            columns_ref.at[position], out_hbm.at[:, :, pl.ds(place, LANES)], sems.at[position]
        )
        copy.start()
        copies.append(copy)
    for copy in copies:
        copy.wait()


def right_products(lefts, pieces, sources, order, first, width, so_far):
    carried = so_far is not None
    many = len(sources)
    vmem = pl.BlockSpec(memory_space=pltpu.VMEM)
    hbm = pl.BlockSpec(memory_space=pltpu.HBM)
    return pl.pallas_call(
        functools.partial(right_kernel, sources, order, first, carried),
        out_shape=jax.ShapeDtypeStruct((AGG_DEV, BLK, width), jnp.float32),
        in_specs=[vmem] * (1 + len(pieces)) + [hbm] * carried,
        out_specs=hbm,
        scratch_shapes=[
            pltpu.VMEM((many, AGG_DEV, BLK, LANES), jnp.float32),
            pltpu.SemaphoreType.DMA((many,)),
        ],
        input_output_aliases={1 + len(pieces): 0} if carried else {},
        compiler_params=pltpu.CompilerParams(vmem_limit_bytes=8 * MIB),
        cost_estimate=pl.CostEstimate(
            flops=2 * many * (AGG_DEV * BLK) ** 2 * PAIRS * LANES,
            bytes_accessed=many * MIB // 16,
            transcendentals=0,
        ),
        name="right_products",
    )(lefts, *pieces, *([so_far] if carried else []))


def paired_plan(columns, counts, aggregate, matrix_blocks, payload, row_count):
    ring = [(i, (i + 1) % row_count) for i in range(row_count)]
    across = [(0, 1), (1, 0)]
    evens = [(i, i ^ 1) for i in range(row_count)]
    odds = [(i, i + 1) for i in range(1, row_count - 1, 2)]
    odds = odds + [(b, a) for a, b in odds] + [(0, 0), (row_count - 1, row_count - 1)]
    crossed = [(2 * a + c, 2 * b + 1 - c) for a, b in odds for c in range(2)]

    def order():
        c, row = lax.axis_index("cols"), lax.axis_index("rows")
        up = 1 - lax.rem(row, 2)
        inside = [row > 0, None, row < row_count - 1]
        spots = [(1, c), (1, 1 - c), (0, c), (2, c), (2 * up, 1 - c), (2 - 2 * up, 1 - c)]
        far = (up == 0) & (row < row_count - 1) | (up == 1) & (row > 0)
        return [(2 * slab + col, live) for (slab, col), live in zip(spots, [None, None, inside[0], inside[2], None, far])]

    far = lax.ppermute(payload, ("rows", "cols"), crossed)
    beside = lax.ppermute(payload, "cols", across)
    below = lax.ppermute(payload, "rows", ring)
    above = lax.ppermute(payload, "rows", [(b, a) for a, b in ring])
    lefts = left_sums(columns, counts, aggregate, payload, matrix_blocks, 6, order)
    lefts, beside = lax.optimization_barrier((lefts, beside))
    inner = lax.ppermute(beside, "rows", evens)
    return right_products(
        lefts,
        [payload, beside, below, above, inner, far],
        [(index, 0) for index in range(6)],
        order,
        0,
        6 * LANES,
        None,
    )


def general_plan(columns, counts, aggregate, matrix_blocks, payload, row_count, col_count):
    forward = [(i, i + 1) for i in range(row_count - 1)]
    backward = [(b, a) for a, b in forward]
    slab = lax.all_gather(payload, "cols", axis=0, tiled=True)
    pieces = [lax.ppermute(slab, "rows", forward), slab, lax.ppermute(slab, "rows", backward)]
    total = 3 * col_count
    order = lambda: [(block, None) for block in range(total)]
    lefts = left_sums(columns, counts, aggregate, payload, matrix_blocks, total, lambda: None)
    sources = [(slab, c * PAYLOAD) for slab in range(3) for c in range(col_count)]
    return right_products(lefts, pieces, sources, order, 0, total * LANES, None)


def per_device(matrix_blocks, restrict, columns, counts, aggregate):
    col_count = lax.axis_size("cols")
    row_count = lax.axis_size("rows")
    payload = pack(aggregate, restrict)
    if col_count == 2 and row_count % 2 == 0:
        return paired_plan(columns, counts, aggregate, matrix_blocks, payload, row_count)
    return general_plan(
        columns, counts, aggregate, matrix_blocks, payload, row_count, col_count
    )


def solution(mesh):
    return jax.shard_map(
        per_device,
        mesh=mesh,
        in_specs=(
            P(("rows", "cols"), None, None),
            P(("rows", "cols"), None),
            P(("rows", "cols"), None),
            P(("rows", "cols")),
            P(("rows", "cols")),
        ),
        out_specs=P(("rows", "cols"), None, None),
        check_vma=False,
    )
```

```python
import functools

import jax
import jax.numpy as jnp
from jax import lax
from jax.experimental import pallas as pl
from jax.experimental.pallas import tpu as pltpu
from jax.sharding import PartitionSpec as P

BLK = 64
SLOTS = 27
ROWS_DEV = 32
AGG_DEV = 2

LANES = 2 * BLK
PAIRS = ROWS_DEV // 2
TAGS = PAIRS * BLK
PAYLOAD = TAGS + PAIRS
STEP = 4
BATCH = 4
CHUNK = 6
MIB = 1 << 20


def pack_kernel(aggregate_hbm, restrict_hbm, out_ref, restrict_ref, wide_ref, aggregate_ref, sems):
    rows = pltpu.make_async_copy(restrict_hbm, restrict_ref, sems.at[0])
    tags = pltpu.make_async_copy(aggregate_hbm, aggregate_ref, sems.at[1])
    rows.start()
    tags.start()
    tags.wait()
    row = lax.broadcasted_iota(jnp.int32, (PAIRS, LANES), 0)
    low = lax.broadcasted_iota(jnp.int32, (PAIRS, LANES), 1) < BLK
    owners = jnp.zeros((PAIRS, LANES), jnp.int32)
    for p in range(PAIRS):
        owner = jnp.where(low, aggregate_ref[p], aggregate_ref[p + PAIRS])
        owners = jnp.where(row == p, owner, owners)
    out_ref[TAGS:, :] = owners.astype(jnp.float32).astype(jnp.bfloat16)
    rows.wait()
    for t in range(BLK // 2):
        x = restrict_ref[:, t * LANES : (t + 1) * LANES].astype(jnp.float32)
        first, second = x[:PAIRS], x[PAIRS:]
        even = jnp.where(low, first, pltpu.roll(second, BLK, 1))
        odd = jnp.where(low, pltpu.roll(first, BLK, 1), second)
        wide_ref[pl.ds(2 * t, PAIRS, stride=BLK), :] = even
        wide_ref[pl.ds(2 * t + 1, PAIRS, stride=BLK), :] = odd
    out_ref[:TAGS, :] = wide_ref[...].astype(jnp.bfloat16)


def pack(aggregate, restrict):
    hbm = pl.BlockSpec(memory_space=pltpu.HBM)
    return pl.pallas_call(
        pack_kernel,
        out_shape=jax.ShapeDtypeStruct((PAYLOAD, LANES), jnp.bfloat16),
        in_specs=[hbm, hbm],
        out_specs=pl.BlockSpec(memory_space=pltpu.VMEM),
        scratch_shapes=[
            pltpu.VMEM(restrict.shape, restrict.dtype),
            pltpu.VMEM((PAIRS * BLK, LANES), jnp.float32),
            pltpu.SMEM(aggregate.shape, aggregate.dtype),
            pltpu.SemaphoreType.DMA((2,)),
        ],
        compiler_params=pltpu.CompilerParams(vmem_limit_bytes=8 * MIB),
        name="pack_payload",
    )(*(pltpu.with_memory_space_constraint(x, pltpu.HBM) for x in (aggregate, restrict)))


def left_kernel(
    order,
    columns_hbm,
    counts_hbm,
    aggregate_hbm,
    payload_ref,
    matrix_hbm,
    out_ref,
    matrix_ref,
    sums_ref,
    columns_ref,
    counts_ref,
    aggregate_ref,
    matrix_sems,
    sems,
):
    total = out_ref.shape[0]
    blocks = CHUNK if total % CHUNK == 0 else CHUNK // 2
    width = blocks * ROWS_DEV
    places = order()
    short = BLK // 2
    steps = PAIRS // STEP

    def rows_copy(step):
        cut = pl.ds(step * STEP, STEP)
        return pltpu.make_async_copy(
            matrix_hbm.at[:, cut], matrix_ref.at[:, cut], matrix_sems.at[step]
        )

    small = [
        pltpu.make_async_copy(columns_hbm, columns_ref, sems.at[0]),
        pltpu.make_async_copy(counts_hbm, counts_ref, sems.at[1]),
        pltpu.make_async_copy(aggregate_hbm, aggregate_ref, sems.at[2]),
    ]
    for copy in small:
        copy.start()
    for step in range(steps):
        rows_copy(step).start()
    low = lax.broadcasted_iota(jnp.int32, (BLK, LANES), 1) < BLK
    low_short = lax.broadcasted_iota(jnp.int32, (short, LANES), 1) < BLK

    def add_all(entries):
        entries = list(entries)
        for first in range(0, len(entries), BATCH):
            batch = entries[first : first + BATCH]
            values = [sums_ref[place] for place, _ in batch]
            for n, (place, tile) in enumerate(batch):
                for earlier in range(n):
                    values[n] = jnp.where(place == batch[earlier][0], values[earlier], values[n])
                values[n] = values[n] + tile
            for (place, _), value in zip(batch, values):
                sums_ref[place] = value

    def tiles_of(base, pair):
        both = payload_ref[pl.ds(pl.multiple_of(pair * BLK, BLK), BLK), :]
        zero = jnp.zeros_like(both)
        lhs = jnp.concatenate([jnp.where(low, both, zero), jnp.where(low, zero, both)], axis=0)
        rows = (pair, pair + PAIRS)
        count = [counts_ref[row] for row in rows]
        offset = [aggregate_ref[row] * width for row in rows]

        def place_of(r, k):
            local = columns_ref[rows[r], k]
            live = k < count[r]
            if total > blocks:
                local = local - base
                live = live & (local >= 0) & (local < width)
            return jnp.where(live, offset[r] + local, AGG_DEV * width)

        for first in range(0, SLOTS, 4):
            many = min(4, SLOTS - first)
            cut = slice(first * BLK, (first + many) * BLK)
            rhs = jnp.concatenate(
                [matrix_ref[0, pair, :, cut], matrix_ref[1, pair, :, cut]], axis=0
            )
            if many * BLK % LANES:
                rhs = jnp.concatenate([rhs, rhs[:, -BLK:]], axis=1)
            left = jnp.dot(lhs, rhs, preferred_element_type=jnp.float32).astype(jnp.bfloat16)
            for k in range(0, many, 2):
                for r in range(2):
                    lanes = slice(k * BLK, (k + 2) * BLK)
                    upper = left[r * BLK : r * BLK + short, lanes]
                    lower = left[r * BLK + short : (r + 1) * BLK, lanes]
                    one = jnp.where(low_short, upper, pltpu.roll(lower, BLK, 1))
                    yield place_of(r, first + k), one.astype(jnp.float32)
                    if k + 1 < many:
                        two = jnp.where(low_short, pltpu.roll(upper, BLK, 1), lower)
                        yield place_of(r, first + k + 1), two.astype(jnp.float32)

    def one_chunk(chunk, first_chunk):
        base = chunk * width
        sums_ref[...] = jnp.zeros_like(sums_ref)
        if first_chunk:
            for copy in small:
                copy.wait()

        def one_step(step, carry):
            if first_chunk:
                rows_copy(step).wait()
            add_all(
                entry for local in range(STEP) for entry in tiles_of(base, step * STEP + local)
            )
            return carry

        lax.fori_loop(0, steps, one_step, 0)
        for position in range(blocks):
            spot, live = places[position] if places is not None else (position, None)
            start = spot * ROWS_DEV
            for a in range(AGG_DEV):
                for p in range(PAIRS):
                    g = a * width + start + p
                    one, two = sums_ref[g], sums_ref[g + PAIRS]
                    if live is not None:
                        one, two = jnp.where(live, one, 0.0), jnp.where(live, two, 0.0)
                    one, two = one.astype(jnp.bfloat16), two.astype(jnp.bfloat16)
                    lanes = slice(p * LANES, (p + 1) * LANES)
                    out_ref[chunk * blocks + position, a * BLK : a * BLK + short, lanes] = (
                        jnp.where(low_short, one, pltpu.roll(two, BLK, 1))
                    )
                    out_ref[
                        chunk * blocks + position, a * BLK + short : (a + 1) * BLK, lanes
                    ] = jnp.where(low_short, pltpu.roll(one, BLK, 1), two)

    one_chunk(0, True)
    if total > blocks:

        def later(chunk, carry):
            one_chunk(chunk, False)
            return carry

        lax.fori_loop(1, total // blocks, later, 0)


def left_sums(columns, counts, aggregate, payload, matrix_blocks, total, order):
    blocks = CHUNK if total % CHUNK == 0 else CHUNK // 2
    matrix = matrix_blocks.reshape(2, PAIRS, BLK, SLOTS * BLK)
    hbm = pl.BlockSpec(memory_space=pltpu.HBM)
    vmem = pl.BlockSpec(memory_space=pltpu.VMEM)
    return pl.pallas_call(
        functools.partial(left_kernel, order),
        out_shape=jax.ShapeDtypeStruct((total, AGG_DEV * BLK, PAIRS * LANES), jnp.bfloat16),
        in_specs=[hbm, hbm, hbm, vmem, hbm],
        out_specs=vmem,
        scratch_shapes=[
            pltpu.VMEM(matrix.shape, matrix.dtype),
            pltpu.VMEM((AGG_DEV * blocks * ROWS_DEV + 1, BLK // 2, LANES), jnp.float32),
            pltpu.SMEM(columns.shape, columns.dtype),
            pltpu.SMEM(counts.shape, counts.dtype),
            pltpu.SMEM(aggregate.shape, aggregate.dtype),
            pltpu.SemaphoreType.DMA((PAIRS // STEP,)),
            pltpu.SemaphoreType.DMA((3,)),
        ],
        compiler_params=pltpu.CompilerParams(vmem_limit_bytes=20 * MIB),
        cost_estimate=pl.CostEstimate(
            flops=4 * ROWS_DEV * SLOTS * BLK**3, bytes_accessed=4 * MIB // 2, transcendentals=0
        ),
        name="left_sums",
    )(
        *(pltpu.with_memory_space_constraint(x, pltpu.HBM) for x in (columns, counts, aggregate)),
        payload,
        pltpu.with_memory_space_constraint(matrix, pltpu.HBM),
    )


def block_product(lefts, piece):
    tags = piece[TAGS:, :].astype(jnp.float32)
    masks = [(tags == j).astype(jnp.float32).astype(jnp.bfloat16) for j in range(AGG_DEV)]
    rhs = jnp.concatenate(
        [
            jnp.concatenate(
                [piece[p * BLK : (p + 1) * BLK, :] * masks[j][p : p + 1, :] for p in range(PAIRS)],
                axis=1,
            )
            for j in range(AGG_DEV)
        ],
        axis=0,
    )
    return lax.dot_general(
        lefts, rhs, (((1,), (1,)), ((), ())), preferred_element_type=jnp.float32
    )


def near_kernel(first, lefts_ref, *refs):
    out_ref = refs[-1]
    for position, piece in enumerate(refs[:-1]):
        total = block_product(lefts_ref[first + position], piece[...])
        for a in range(AGG_DEV):
            out_ref[position, a] = total[a * BLK : (a + 1) * BLK]


def near_products(lefts, pieces, first):
    many = len(pieces)
    vmem = pl.BlockSpec(memory_space=pltpu.VMEM)
    return pl.pallas_call(
        functools.partial(near_kernel, first),
        out_shape=jax.ShapeDtypeStruct((many, AGG_DEV, BLK, LANES), jnp.float32),
        in_specs=[vmem] * (1 + many),
        out_specs=vmem,
        compiler_params=pltpu.CompilerParams(vmem_limit_bytes=8 * MIB),
        cost_estimate=right_cost(many),
        name="near_products",
    )(lefts, *pieces)


def right_cost(many):
    return pl.CostEstimate(
        flops=2 * many * (AGG_DEV * BLK) ** 2 * PAIRS * LANES,
        bytes_accessed=many * MIB // 16,
        transcendentals=0,
    )


def right_kernel(sources, order, first, lefts_ref, *refs):
    out_hbm, columns_ref, sems = refs[-3:]
    copies = []

    def send(position, tile):
        place, _ = order()[position]
        place = place * LANES if isinstance(place, int) else pl.multiple_of(place * LANES, LANES)
        copy = pltpu.make_async_copy(
            tile, out_hbm.at[:, :, pl.ds(place, LANES)], sems.at[position]
        )
        copy.start()
        copies.append(copy)

    for position in range(first):
        send(position, refs[-4].at[position])
    for position, (index, start) in enumerate(sources):
        total = block_product(
            lefts_ref[first + position], refs[index][start : start + PAYLOAD, :]
        )
        for a in range(AGG_DEV):
            columns_ref[position, a] = total[a * BLK : (a + 1) * BLK]
        send(first + position, columns_ref.at[position])
    for copy in copies:
        copy.wait()


def right_products(lefts, pieces, sources, order, width, near):
    first = 0 if near is None else near.shape[0]
    many = len(sources)
    vmem = pl.BlockSpec(memory_space=pltpu.VMEM)
    return pl.pallas_call(
        functools.partial(right_kernel, sources, order, first),
        out_shape=jax.ShapeDtypeStruct((AGG_DEV, BLK, width), jnp.float32),
        in_specs=[vmem] * (1 + len(pieces) + (first > 0)),
        out_specs=pl.BlockSpec(memory_space=pltpu.HBM),
        scratch_shapes=[
            pltpu.VMEM((many, AGG_DEV, BLK, LANES), jnp.float32),
            pltpu.SemaphoreType.DMA((first + many,)),
        ],
        compiler_params=pltpu.CompilerParams(vmem_limit_bytes=8 * MIB),
        cost_estimate=right_cost(many),
        name="right_products",
    )(lefts, *pieces, *([near] if first else []))


def paired_plan(columns, counts, aggregate, matrix_blocks, payload, row_count):
    ring = [(i, (i + 1) % row_count) for i in range(row_count)]
    across = [(0, 1), (1, 0)]
    evens = [(i, i ^ 1) for i in range(row_count)]
    odds = [(i, i + 1) for i in range(1, row_count - 1, 2)]
    odds = odds + [(b, a) for a, b in odds] + [(0, 0), (row_count - 1, row_count - 1)]
    crossed = [(2 * a + c, 2 * b + 1 - c) for a, b in odds for c in range(2)]

    def order():
        c, row = lax.axis_index("cols"), lax.axis_index("rows")
        up = 1 - lax.rem(row, 2)
        low, high = row > 0, row < row_count - 1
        far = (up == 0) & high | (up == 1) & low
        return [
            (2 + c, None),
            (3 - c, None),
            (4 - 4 * up + 1 - c, far),
            (4 * up + 1 - c, None),
            (c, low),
            (4 + c, high),
        ]

    far = lax.ppermute(payload, ("rows", "cols"), crossed)
    beside = lax.ppermute(payload, "cols", across)
    below = lax.ppermute(payload, "rows", ring)
    above = lax.ppermute(payload, "rows", [(b, a) for a, b in ring])
    lefts = left_sums(columns, counts, aggregate, payload, matrix_blocks, 6, order)
    lefts, beside = lax.optimization_barrier((lefts, beside))
    inner = lax.ppermute(beside, "rows", evens)
    near = near_products(lefts, [payload, beside, far], 0)
    sources = [(index, 0) for index in range(3)]
    return right_products(lefts, [inner, below, above], sources, order, 6 * LANES, near)


def general_plan(columns, counts, aggregate, matrix_blocks, payload, row_count, col_count):
    forward = [(i, i + 1) for i in range(row_count - 1)]
    backward = [(b, a) for a, b in forward]
    slab = lax.all_gather(payload, "cols", axis=0, tiled=True)
    pieces = [lax.ppermute(slab, "rows", forward), slab, lax.ppermute(slab, "rows", backward)]
    total = 3 * col_count
    order = lambda: [(block, None) for block in range(total)]
    lefts = left_sums(columns, counts, aggregate, payload, matrix_blocks, total, lambda: None)
    sources = [(slab, c * PAYLOAD) for slab in range(3) for c in range(col_count)]
    return right_products(lefts, pieces, sources, order, total * LANES, None)


def per_device(matrix_blocks, restrict, columns, counts, aggregate):
    col_count = lax.axis_size("cols")
    row_count = lax.axis_size("rows")
    payload = pack(aggregate, restrict)
    if col_count == 2 and row_count % 2 == 0:
        return paired_plan(columns, counts, aggregate, matrix_blocks, payload, row_count)
    return general_plan(
        columns, counts, aggregate, matrix_blocks, payload, row_count, col_count
    )


def solution(mesh):
    return jax.shard_map(
        per_device,
        mesh=mesh,
        in_specs=(
            P(("rows", "cols"), None, None),
            P(("rows", "cols"), None),
            P(("rows", "cols"), None),
            P(("rows", "cols")),
            P(("rows", "cols")),
        ),
        out_specs=P(("rows", "cols"), None, None),
        check_vma=False,
    )
```

```python
import functools

import jax
import jax.numpy as jnp
from jax import lax
from jax.experimental import pallas as pl
from jax.experimental.pallas import tpu as pltpu
from jax.sharding import PartitionSpec as P

BLK = 64
SLOTS = 27
ROWS_DEV = 32
AGG_DEV = 2

LANES = 2 * BLK
PAIRS = ROWS_DEV // 2
TAGS = PAIRS * BLK
PAYLOAD = TAGS + PAIRS
STEP = 4
BATCH = 4
CHUNK = 6
MIB = 1 << 20


def pack_kernel(aggregate_hbm, restrict_hbm, out_ref, restrict_ref, aggregate_ref, sems):
    rows = pltpu.make_async_copy(restrict_hbm, restrict_ref, sems.at[0])
    tags = pltpu.make_async_copy(aggregate_hbm, aggregate_ref, sems.at[1])
    rows.start()
    tags.start()
    tags.wait()
    row = lax.broadcasted_iota(jnp.int32, (PAIRS, LANES), 0)
    low = lax.broadcasted_iota(jnp.int32, (PAIRS, LANES), 1) < BLK
    owners = jnp.zeros((PAIRS, LANES), jnp.int32)
    for p in range(PAIRS):
        owner = jnp.where(low, aggregate_ref[p], aggregate_ref[p + PAIRS])
        owners = jnp.where(row == p, owner, owners)
    out_ref[TAGS:, :] = owners.astype(jnp.float32).astype(jnp.bfloat16)
    rows.wait()
    halves = []
    for t in range(BLK // 2):
        x = restrict_ref[:, t * LANES : (t + 1) * LANES].astype(jnp.float32)
        first, second = x[:PAIRS], x[PAIRS:]
        halves.append(jnp.where(low, first, pltpu.roll(second, BLK, 1)))
        halves.append(jnp.where(low, pltpu.roll(first, BLK, 1), second))
    blocks = jnp.stack(halves, axis=0).swapaxes(0, 1).reshape(TAGS, LANES)
    out_ref[:TAGS, :] = blocks.astype(jnp.bfloat16)


def pack(aggregate, restrict):
    hbm = pl.BlockSpec(memory_space=pltpu.HBM)
    return pl.pallas_call(
        pack_kernel,
        out_shape=jax.ShapeDtypeStruct((PAYLOAD, LANES), jnp.bfloat16),
        in_specs=[hbm, hbm],
        out_specs=pl.BlockSpec(memory_space=pltpu.VMEM),
        scratch_shapes=[
            pltpu.VMEM(restrict.shape, restrict.dtype),
            pltpu.SMEM(aggregate.shape, aggregate.dtype),
            pltpu.SemaphoreType.DMA((2,)),
        ],
        compiler_params=pltpu.CompilerParams(vmem_limit_bytes=8 * MIB),
        name="pack_payload",
    )(*(pltpu.with_memory_space_constraint(x, pltpu.HBM) for x in (aggregate, restrict)))


def left_kernel(
    order,
    columns_hbm,
    counts_hbm,
    aggregate_hbm,
    payload_ref,
    matrix_hbm,
    out_ref,
    matrix_ref,
    sums_ref,
    columns_ref,
    counts_ref,
    aggregate_ref,
    matrix_sems,
    sems,
):
    total = out_ref.shape[0]
    blocks = CHUNK if total % CHUNK == 0 else CHUNK // 2
    width = blocks * ROWS_DEV
    places = order()
    short = BLK // 2
    steps = PAIRS // STEP

    def rows_copy(step):
        cut = pl.ds(step * STEP, STEP)
        return pltpu.make_async_copy(
            matrix_hbm.at[:, cut], matrix_ref.at[:, cut], matrix_sems.at[step]
        )

    small = [
        pltpu.make_async_copy(columns_hbm, columns_ref, sems.at[0]),
        pltpu.make_async_copy(counts_hbm, counts_ref, sems.at[1]),
        pltpu.make_async_copy(aggregate_hbm, aggregate_ref, sems.at[2]),
    ]
    for copy in small:
        copy.start()
    for step in range(steps):
        rows_copy(step).start()
    low = lax.broadcasted_iota(jnp.int32, (BLK, LANES), 1) < BLK
    low_short = lax.broadcasted_iota(jnp.int32, (short, LANES), 1) < BLK

    def add_all(entries):
        entries = list(entries)
        for first in range(0, len(entries), BATCH):
            batch = entries[first : first + BATCH]
            values = [sums_ref[place] for place, _ in batch]
            for n, (place, tile) in enumerate(batch):
                for earlier in range(n):
                    values[n] = jnp.where(place == batch[earlier][0], values[earlier], values[n])
                values[n] = values[n] + tile
            for (place, _), value in zip(batch, values):
                sums_ref[place] = value

    def tiles_of(base, pair):
        both = payload_ref[pl.ds(pl.multiple_of(pair * BLK, BLK), BLK), :]
        zero = jnp.zeros_like(both)
        lhs = jnp.concatenate([jnp.where(low, both, zero), jnp.where(low, zero, both)], axis=0)
        rows = (pair, pair + PAIRS)
        count = [counts_ref[row] for row in rows]
        offset = [aggregate_ref[row] * width for row in rows]

        def place_of(r, k):
            local = columns_ref[rows[r], k]
            live = k < count[r]
            if total > blocks:
                local = local - base
                live = live & (local >= 0) & (local < width)
            return jnp.where(live, offset[r] + local, AGG_DEV * width)

        for first in range(0, SLOTS, 4):
            many = min(4, SLOTS - first)
            cut = slice(first * BLK, (first + many) * BLK)
            rhs = jnp.concatenate(
                [matrix_ref[0, pair, :, cut], matrix_ref[1, pair, :, cut]], axis=0
            )
            if many * BLK % LANES:
                rhs = jnp.concatenate([rhs, rhs[:, -BLK:]], axis=1)
            left = jnp.dot(lhs, rhs, preferred_element_type=jnp.float32).astype(jnp.bfloat16)
            for k in range(0, many, 2):
                for r in range(2):
                    lanes = slice(k * BLK, (k + 2) * BLK)
                    upper = left[r * BLK : r * BLK + short, lanes]
                    lower = left[r * BLK + short : (r + 1) * BLK, lanes]
                    one = jnp.where(low_short, upper, pltpu.roll(lower, BLK, 1))
                    yield place_of(r, first + k), one.astype(jnp.float32)
                    if k + 1 < many:
                        two = jnp.where(low_short, pltpu.roll(upper, BLK, 1), lower)
                        yield place_of(r, first + k + 1), two.astype(jnp.float32)

    def one_chunk(chunk, first_chunk):
        base = chunk * width
        sums_ref[...] = jnp.zeros_like(sums_ref)
        if first_chunk:
            for copy in small:
                copy.wait()

        def one_step(step, carry):
            if first_chunk:
                rows_copy(step).wait()
            add_all(
                entry for local in range(STEP) for entry in tiles_of(base, step * STEP + local)
            )
            return carry

        lax.fori_loop(0, steps, one_step, 0)
        for position in range(blocks):
            spot, live = places[position] if places is not None else (position, None)
            start = spot * ROWS_DEV
            for a in range(AGG_DEV):
                for p in range(PAIRS):
                    g = a * width + start + p
                    one, two = sums_ref[g], sums_ref[g + PAIRS]
                    if live is not None:
                        one, two = jnp.where(live, one, 0.0), jnp.where(live, two, 0.0)
                    one, two = one.astype(jnp.bfloat16), two.astype(jnp.bfloat16)
                    lanes = slice(p * LANES, (p + 1) * LANES)
                    out_ref[chunk * blocks + position, a * BLK : a * BLK + short, lanes] = (
                        jnp.where(low_short, one, pltpu.roll(two, BLK, 1))
                    )
                    out_ref[
                        chunk * blocks + position, a * BLK + short : (a + 1) * BLK, lanes
                    ] = jnp.where(low_short, pltpu.roll(one, BLK, 1), two)

    one_chunk(0, True)
    if total > blocks:

        def later(chunk, carry):
            one_chunk(chunk, False)
            return carry

        lax.fori_loop(1, total // blocks, later, 0)


def left_sums(columns, counts, aggregate, payload, matrix_blocks, total, order):
    blocks = CHUNK if total % CHUNK == 0 else CHUNK // 2
    matrix = matrix_blocks.reshape(2, PAIRS, BLK, SLOTS * BLK)
    hbm = pl.BlockSpec(memory_space=pltpu.HBM)
    vmem = pl.BlockSpec(memory_space=pltpu.VMEM)
    return pl.pallas_call(
        functools.partial(left_kernel, order),
        out_shape=jax.ShapeDtypeStruct((total, AGG_DEV * BLK, PAIRS * LANES), jnp.bfloat16),
        in_specs=[hbm, hbm, hbm, vmem, hbm],
        out_specs=vmem,
        scratch_shapes=[
            pltpu.VMEM(matrix.shape, matrix.dtype),
            pltpu.VMEM((AGG_DEV * blocks * ROWS_DEV + 1, BLK // 2, LANES), jnp.float32),
            pltpu.SMEM(columns.shape, columns.dtype),
            pltpu.SMEM(counts.shape, counts.dtype),
            pltpu.SMEM(aggregate.shape, aggregate.dtype),
            pltpu.SemaphoreType.DMA((PAIRS // STEP,)),
            pltpu.SemaphoreType.DMA((3,)),
        ],
        compiler_params=pltpu.CompilerParams(vmem_limit_bytes=20 * MIB),
        cost_estimate=pl.CostEstimate(
            flops=4 * ROWS_DEV * SLOTS * BLK**3, bytes_accessed=4 * MIB // 2, transcendentals=0
        ),
        name="left_sums",
    )(
        *(pltpu.with_memory_space_constraint(x, pltpu.HBM) for x in (columns, counts, aggregate)),
        payload,
        pltpu.with_memory_space_constraint(matrix, pltpu.HBM),
    )


def block_product(lefts, piece):
    tags = piece[TAGS:, :].astype(jnp.float32)
    masks = [(tags == j).astype(jnp.float32).astype(jnp.bfloat16) for j in range(AGG_DEV)]
    rhs = jnp.concatenate(
        [
            jnp.concatenate(
                [piece[p * BLK : (p + 1) * BLK, :] * masks[j][p : p + 1, :] for p in range(PAIRS)],
                axis=1,
            )
            for j in range(AGG_DEV)
        ],
        axis=0,
    )
    return lax.dot_general(
        lefts, rhs, (((1,), (1,)), ((), ())), preferred_element_type=jnp.float32
    )


def near_kernel(first, lefts_ref, *refs):
    out_ref = refs[-1]
    for position, piece in enumerate(refs[:-1]):
        total = block_product(lefts_ref[first + position], piece[...])
        for a in range(AGG_DEV):
            out_ref[position, a] = total[a * BLK : (a + 1) * BLK]


def near_products(lefts, pieces, first):
    many = len(pieces)
    vmem = pl.BlockSpec(memory_space=pltpu.VMEM)
    return pl.pallas_call(
        functools.partial(near_kernel, first),
        out_shape=jax.ShapeDtypeStruct((many, AGG_DEV, BLK, LANES), jnp.float32),
        in_specs=[vmem] * (1 + many),
        out_specs=vmem,
        compiler_params=pltpu.CompilerParams(vmem_limit_bytes=8 * MIB),
        cost_estimate=right_cost(many),
        name="near_products",
    )(lefts, *pieces)


def right_cost(many):
    return pl.CostEstimate(
        flops=2 * many * (AGG_DEV * BLK) ** 2 * PAIRS * LANES,
        bytes_accessed=many * MIB // 16,
        transcendentals=0,
    )


def right_kernel(sources, order, first, lefts_ref, *refs):
    out_hbm, columns_ref, sems = refs[-3:]
    copies = []

    def send(position, tile):
        place, _ = order()[position]
        place = place * LANES if isinstance(place, int) else pl.multiple_of(place * LANES, LANES)
        copy = pltpu.make_async_copy(
            tile, out_hbm.at[:, :, pl.ds(place, LANES)], sems.at[position]
        )
        copy.start()
        copies.append(copy)

    for position in range(first):
        send(position, refs[-4].at[position])
    for position, (index, start) in enumerate(sources):
        total = block_product(
            lefts_ref[first + position], refs[index][start : start + PAYLOAD, :]
        )
        for a in range(AGG_DEV):
            columns_ref[position, a] = total[a * BLK : (a + 1) * BLK]
        send(first + position, columns_ref.at[position])
    for copy in copies:
        copy.wait()


def right_products(lefts, pieces, sources, order, width, near):
    first = 0 if near is None else near.shape[0]
    many = len(sources)
    vmem = pl.BlockSpec(memory_space=pltpu.VMEM)
    return pl.pallas_call(
        functools.partial(right_kernel, sources, order, first),
        out_shape=jax.ShapeDtypeStruct((AGG_DEV, BLK, width), jnp.float32),
        in_specs=[vmem] * (1 + len(pieces) + (first > 0)),
        out_specs=pl.BlockSpec(memory_space=pltpu.HBM),
        scratch_shapes=[
            pltpu.VMEM((many, AGG_DEV, BLK, LANES), jnp.float32),
            pltpu.SemaphoreType.DMA((first + many,)),
        ],
        compiler_params=pltpu.CompilerParams(vmem_limit_bytes=8 * MIB),
        cost_estimate=right_cost(many),
        name="right_products",
    )(lefts, *pieces, *([near] if first else []))


def paired_plan(columns, counts, aggregate, matrix_blocks, payload, row_count):
    ring = [(i, (i + 1) % row_count) for i in range(row_count)]
    across = [(0, 1), (1, 0)]
    evens = [(i, i ^ 1) for i in range(row_count)]
    odds = [(i, i + 1) for i in range(1, row_count - 1, 2)]
    odds = odds + [(b, a) for a, b in odds] + [(0, 0), (row_count - 1, row_count - 1)]
    crossed = [(2 * a + c, 2 * b + 1 - c) for a, b in odds for c in range(2)]

    def order():
        c, row = lax.axis_index("cols"), lax.axis_index("rows")
        up = 1 - lax.rem(row, 2)
        low, high = row > 0, row < row_count - 1
        far = (up == 0) & high | (up == 1) & low
        return [
            (2 + c, None),
            (3 - c, None),
            (4 - 4 * up + 1 - c, far),
            (4 * up + 1 - c, None),
            (c, low),
            (4 + c, high),
        ]

    far = lax.ppermute(payload, ("rows", "cols"), crossed)
    beside = lax.ppermute(payload, "cols", across)
    below = lax.ppermute(payload, "rows", ring)
    above = lax.ppermute(payload, "rows", [(b, a) for a, b in ring])
    lefts = left_sums(columns, counts, aggregate, payload, matrix_blocks, 6, order)
    lefts, beside = lax.optimization_barrier((lefts, beside))
    inner = lax.ppermute(beside, "rows", evens)
    near = near_products(lefts, [payload, beside, far], 0)
    sources = [(index, 0) for index in range(3)]
    return right_products(lefts, [inner, below, above], sources, order, 6 * LANES, near)


def general_plan(columns, counts, aggregate, matrix_blocks, payload, row_count, col_count):
    forward = [(i, i + 1) for i in range(row_count - 1)]
    backward = [(b, a) for a, b in forward]
    slab = lax.all_gather(payload, "cols", axis=0, tiled=True)
    pieces = [lax.ppermute(slab, "rows", forward), slab, lax.ppermute(slab, "rows", backward)]
    total = 3 * col_count
    order = lambda: [(block, None) for block in range(total)]
    lefts = left_sums(columns, counts, aggregate, payload, matrix_blocks, total, lambda: None)
    sources = [(slab, c * PAYLOAD) for slab in range(3) for c in range(col_count)]
    return right_products(lefts, pieces, sources, order, total * LANES, None)


def per_device(matrix_blocks, restrict, columns, counts, aggregate):
    col_count = lax.axis_size("cols")
    row_count = lax.axis_size("rows")
    payload = pack(aggregate, restrict)
    if col_count == 2 and row_count % 2 == 0:
        return paired_plan(columns, counts, aggregate, matrix_blocks, payload, row_count)
    return general_plan(
        columns, counts, aggregate, matrix_blocks, payload, row_count, col_count
    )


def solution(mesh):
    return jax.shard_map(
        per_device,
        mesh=mesh,
        in_specs=(
            P(("rows", "cols"), None, None),
            P(("rows", "cols"), None),
            P(("rows", "cols"), None),
            P(("rows", "cols")),
            P(("rows", "cols")),
        ),
        out_specs=P(("rows", "cols"), None, None),
        check_vma=False,
    )
```

```python
import functools

import jax
import jax.numpy as jnp
from jax import lax
from jax.experimental import pallas as pl
from jax.experimental.pallas import tpu as pltpu
from jax.sharding import PartitionSpec as P

BLK = 64
SLOTS = 27
ROWS_DEV = 32
AGG_DEV = 2

LANES = 2 * BLK
PAIRS = ROWS_DEV // 2
TAGS = PAIRS * BLK
PAYLOAD = TAGS + PAIRS
STEP = 4
BATCH = 4
CHUNK = 6
MIB = 1 << 20


def pack_kernel(aggregate_hbm, restrict_hbm, out_ref, restrict_ref, aggregate_ref, sems):
    rows = pltpu.make_async_copy(restrict_hbm, restrict_ref, sems.at[0])
    tags = pltpu.make_async_copy(aggregate_hbm, aggregate_ref, sems.at[1])
    rows.start()
    tags.start()
    tags.wait()
    row = lax.broadcasted_iota(jnp.int32, (PAIRS, LANES), 0)
    low = lax.broadcasted_iota(jnp.int32, (PAIRS, LANES), 1) < BLK
    owners = jnp.zeros((PAIRS, LANES), jnp.int32)
    for p in range(PAIRS):
        owner = jnp.where(low, aggregate_ref[p], aggregate_ref[p + PAIRS])
        owners = jnp.where(row == p, owner, owners)
    out_ref[TAGS:, :] = owners.astype(jnp.float32).astype(jnp.bfloat16)
    rows.wait()
    halves = []
    for t in range(BLK // 2):
        x = restrict_ref[:, t * LANES : (t + 1) * LANES].astype(jnp.float32)
        first, second = x[:PAIRS], x[PAIRS:]
        halves.append(jnp.where(low, first, pltpu.roll(second, BLK, 1)))
        halves.append(jnp.where(low, pltpu.roll(first, BLK, 1), second))
    blocks = jnp.stack(halves, axis=0).swapaxes(0, 1).reshape(TAGS, LANES)
    out_ref[:TAGS, :] = blocks.astype(jnp.bfloat16)


def pack(aggregate, restrict):
    hbm = pl.BlockSpec(memory_space=pltpu.HBM)
    return pl.pallas_call(
        pack_kernel,
        out_shape=jax.ShapeDtypeStruct((PAYLOAD, LANES), jnp.bfloat16),
        in_specs=[hbm, hbm],
        out_specs=pl.BlockSpec(memory_space=pltpu.VMEM),
        scratch_shapes=[
            pltpu.VMEM(restrict.shape, restrict.dtype),
            pltpu.SMEM(aggregate.shape, aggregate.dtype),
            pltpu.SemaphoreType.DMA((2,)),
        ],
        compiler_params=pltpu.CompilerParams(vmem_limit_bytes=8 * MIB),
        name="pack_payload",
    )(*(pltpu.with_memory_space_constraint(x, pltpu.HBM) for x in (aggregate, restrict)))


def left_kernel(
    order,
    columns_hbm,
    counts_hbm,
    aggregate_hbm,
    payload_ref,
    matrix_hbm,
    out_ref,
    matrix_ref,
    sums_ref,
    columns_ref,
    counts_ref,
    aggregate_ref,
    matrix_sems,
    sems,
):
    total = out_ref.shape[0]
    blocks = CHUNK if total % CHUNK == 0 else CHUNK // 2
    width = blocks * ROWS_DEV
    places = order()
    short = BLK // 2
    steps = PAIRS // STEP

    def rows_copy(step):
        cut = pl.ds(step * STEP, STEP)
        return pltpu.make_async_copy(
            matrix_hbm.at[:, cut], matrix_ref.at[:, cut], matrix_sems.at[step]
        )

    small = [
        pltpu.make_async_copy(columns_hbm, columns_ref, sems.at[0]),
        pltpu.make_async_copy(counts_hbm, counts_ref, sems.at[1]),
        pltpu.make_async_copy(aggregate_hbm, aggregate_ref, sems.at[2]),
    ]
    for copy in small:
        copy.start()
    for step in range(steps):
        rows_copy(step).start()
    low = lax.broadcasted_iota(jnp.int32, (BLK, LANES), 1) < BLK
    low_short = lax.broadcasted_iota(jnp.int32, (short, LANES), 1) < BLK

    def add_all(entries):
        entries = list(entries)
        for first in range(0, len(entries), BATCH):
            batch = entries[first : first + BATCH]
            values = [sums_ref[place] for place, _ in batch]
            for n, (place, tile) in enumerate(batch):
                for earlier in range(n):
                    values[n] = jnp.where(place == batch[earlier][0], values[earlier], values[n])
                values[n] = values[n] + tile
            for (place, _), value in zip(batch, values):
                sums_ref[place] = value

    def tiles_of(base, pair):
        both = payload_ref[pl.ds(pl.multiple_of(pair * BLK, BLK), BLK), :]
        zero = jnp.zeros_like(both)
        lhs = jnp.concatenate([jnp.where(low, both, zero), jnp.where(low, zero, both)], axis=0)
        rows = (pair, pair + PAIRS)
        count = [counts_ref[row] for row in rows]
        offset = [aggregate_ref[row] * width for row in rows]

        def place_of(r, k):
            local = columns_ref[rows[r], k]
            live = k < count[r]
            if total > blocks:
                local = local - base
                live = live & (local >= 0) & (local < width)
            return jnp.where(live, offset[r] + local, AGG_DEV * width)

        for first in range(0, SLOTS, 4):
            many = min(4, SLOTS - first)
            cut = slice(first * BLK, (first + many) * BLK)
            rhs = jnp.concatenate(
                [matrix_ref[0, pair, :, cut], matrix_ref[1, pair, :, cut]], axis=0
            )
            if many * BLK % LANES:
                rhs = jnp.concatenate([rhs, rhs[:, -BLK:]], axis=1)
            left = jnp.dot(lhs, rhs, preferred_element_type=jnp.float32).astype(jnp.bfloat16)
            for k in range(0, many, 2):
                for r in range(2):
                    lanes = slice(k * BLK, (k + 2) * BLK)
                    upper = left[r * BLK : r * BLK + short, lanes]
                    lower = left[r * BLK + short : (r + 1) * BLK, lanes]
                    one = jnp.where(low_short, upper, pltpu.roll(lower, BLK, 1))
                    yield place_of(r, first + k), one.astype(jnp.float32)
                    if k + 1 < many:
                        two = jnp.where(low_short, pltpu.roll(upper, BLK, 1), lower)
                        yield place_of(r, first + k + 1), two.astype(jnp.float32)

    def one_chunk(chunk, first_chunk):
        base = chunk * width
        sums_ref[...] = jnp.zeros_like(sums_ref)
        if first_chunk:
            for copy in small:
                copy.wait()

        def one_step(step, carry):
            if first_chunk:
                rows_copy(step).wait()
            add_all(
                entry for local in range(STEP) for entry in tiles_of(base, step * STEP + local)
            )
            return carry

        lax.fori_loop(0, steps, one_step, 0)
        for position in range(blocks):
            spot, live = places[position] if places is not None else (position, None)
            start = spot * ROWS_DEV
            for a in range(AGG_DEV):
                for p in range(PAIRS):
                    g = a * width + start + p
                    one, two = sums_ref[g], sums_ref[g + PAIRS]
                    if live is not None:
                        one, two = jnp.where(live, one, 0.0), jnp.where(live, two, 0.0)
                    one, two = one.astype(jnp.bfloat16), two.astype(jnp.bfloat16)
                    lanes = slice(p * LANES, (p + 1) * LANES)
                    out_ref[chunk * blocks + position, a * BLK : a * BLK + short, lanes] = (
                        jnp.where(low_short, one, pltpu.roll(two, BLK, 1))
                    )
                    out_ref[
                        chunk * blocks + position, a * BLK + short : (a + 1) * BLK, lanes
                    ] = jnp.where(low_short, pltpu.roll(one, BLK, 1), two)

    one_chunk(0, True)
    if total > blocks:

        def later(chunk, carry):
            one_chunk(chunk, False)
            return carry

        lax.fori_loop(1, total // blocks, later, 0)


def left_sums(columns, counts, aggregate, payload, matrix_blocks, total, order):
    blocks = CHUNK if total % CHUNK == 0 else CHUNK // 2
    matrix = matrix_blocks.reshape(2, PAIRS, BLK, SLOTS * BLK)
    hbm = pl.BlockSpec(memory_space=pltpu.HBM)
    vmem = pl.BlockSpec(memory_space=pltpu.VMEM)
    return pl.pallas_call(
        functools.partial(left_kernel, order),
        out_shape=jax.ShapeDtypeStruct((total, AGG_DEV * BLK, PAIRS * LANES), jnp.bfloat16),
        in_specs=[hbm, hbm, hbm, vmem, hbm],
        out_specs=vmem,
        scratch_shapes=[
            pltpu.VMEM(matrix.shape, matrix.dtype),
            pltpu.VMEM((AGG_DEV * blocks * ROWS_DEV + 1, BLK // 2, LANES), jnp.float32),
            pltpu.SMEM(columns.shape, columns.dtype),
            pltpu.SMEM(counts.shape, counts.dtype),
            pltpu.SMEM(aggregate.shape, aggregate.dtype),
            pltpu.SemaphoreType.DMA((PAIRS // STEP,)),
            pltpu.SemaphoreType.DMA((3,)),
        ],
        compiler_params=pltpu.CompilerParams(vmem_limit_bytes=20 * MIB),
        cost_estimate=pl.CostEstimate(
            flops=4 * ROWS_DEV * SLOTS * BLK**3, bytes_accessed=4 * MIB // 2, transcendentals=0
        ),
        name="left_sums",
    )(
        *(pltpu.with_memory_space_constraint(x, pltpu.HBM) for x in (columns, counts, aggregate)),
        payload,
        pltpu.with_memory_space_constraint(matrix, pltpu.HBM),
    )


def block_product(lefts, piece):
    tags = piece[TAGS:, :].astype(jnp.float32)
    masks = [(tags == j).astype(jnp.float32).astype(jnp.bfloat16) for j in range(AGG_DEV)]
    rhs = jnp.concatenate(
        [
            jnp.concatenate(
                [piece[p * BLK : (p + 1) * BLK, :] * masks[j][p : p + 1, :] for p in range(PAIRS)],
                axis=1,
            )
            for j in range(AGG_DEV)
        ],
        axis=0,
    )
    return lax.dot_general(
        lefts, rhs, (((1,), (1,)), ((), ())), preferred_element_type=jnp.float32
    )


def near_kernel(first, lefts_ref, *refs):
    out_ref = refs[-1]
    for position, piece in enumerate(refs[:-1]):
        total = block_product(lefts_ref[first + position], piece[...])
        for a in range(AGG_DEV):
            out_ref[position, a] = total[a * BLK : (a + 1) * BLK]


def near_products(lefts, pieces, first):
    many = len(pieces)
    vmem = pl.BlockSpec(memory_space=pltpu.VMEM)
    return pl.pallas_call(
        functools.partial(near_kernel, first),
        out_shape=jax.ShapeDtypeStruct((many, AGG_DEV, BLK, LANES), jnp.float32),
        in_specs=[vmem] * (1 + many),
        out_specs=vmem,
        compiler_params=pltpu.CompilerParams(vmem_limit_bytes=8 * MIB),
        cost_estimate=right_cost(many),
        name="near_products",
    )(lefts, *pieces)


def right_cost(many):
    return pl.CostEstimate(
        flops=2 * many * (AGG_DEV * BLK) ** 2 * PAIRS * LANES,
        bytes_accessed=many * MIB // 16,
        transcendentals=0,
    )


def right_kernel(sources, order, first, lefts_ref, *refs):
    out_hbm, columns_ref, sems = refs[-3:]
    copies = []

    def send(position, tile):
        place, _ = order()[position]
        place = place * LANES if isinstance(place, int) else pl.multiple_of(place * LANES, LANES)
        copy = pltpu.make_async_copy(
            tile, out_hbm.at[:, :, pl.ds(place, LANES)], sems.at[position]
        )
        copy.start()
        copies.append(copy)

    for position in range(first):
        send(position, refs[-4].at[position])
    for position, (index, start) in enumerate(sources):
        total = block_product(
            lefts_ref[first + position], refs[index][start : start + PAYLOAD, :]
        )
        for a in range(AGG_DEV):
            columns_ref[position, a] = total[a * BLK : (a + 1) * BLK]
        send(first + position, columns_ref.at[position])
    for copy in copies:
        copy.wait()


def right_products(lefts, pieces, sources, order, width, near):
    first = 0 if near is None else near.shape[0]
    many = len(sources)
    vmem = pl.BlockSpec(memory_space=pltpu.VMEM)
    return pl.pallas_call(
        functools.partial(right_kernel, sources, order, first),
        out_shape=jax.ShapeDtypeStruct((AGG_DEV, BLK, width), jnp.float32),
        in_specs=[vmem] * (1 + len(pieces) + (first > 0)),
        out_specs=pl.BlockSpec(memory_space=pltpu.HBM),
        scratch_shapes=[
            pltpu.VMEM((many, AGG_DEV, BLK, LANES), jnp.float32),
            pltpu.SemaphoreType.DMA((first + many,)),
        ],
        compiler_params=pltpu.CompilerParams(vmem_limit_bytes=8 * MIB),
        cost_estimate=right_cost(many),
        name="right_products",
    )(lefts, *pieces, *([near] if first else []))


def paired_plan(columns, counts, aggregate, matrix_blocks, payload, row_count):
    ring = [(i, (i + 1) % row_count) for i in range(row_count)]
    across = [(0, 1), (1, 0)]
    evens = [(i, i ^ 1) for i in range(row_count)]
    odds = [(i, i + 1) for i in range(1, row_count - 1, 2)]
    odds = odds + [(b, a) for a, b in odds] + [(0, 0), (row_count - 1, row_count - 1)]
    crossed = [(2 * a + c, 2 * b + 1 - c) for a, b in odds for c in range(2)]

    def order():
        c, row = lax.axis_index("cols"), lax.axis_index("rows")
        up = 1 - lax.rem(row, 2)
        low, high = row > 0, row < row_count - 1
        far = (up == 0) & high | (up == 1) & low
        return [
            (2 + c, None),
            (3 - c, None),
            (4 + c, high),
            (c, low),
            (4 * up + 1 - c, None),
            (4 - 4 * up + 1 - c, far),
        ]

    far = lax.ppermute(payload, ("rows", "cols"), crossed)
    beside = lax.ppermute(payload, "cols", across)
    below = lax.ppermute(payload, "rows", ring)
    above = lax.ppermute(payload, "rows", [(b, a) for a, b in ring])
    lefts = left_sums(columns, counts, aggregate, payload, matrix_blocks, 6, order)
    lefts, beside = lax.optimization_barrier((lefts, beside))
    inner = lax.ppermute(beside, "rows", evens)
    near = near_products(lefts, [payload, beside, above, below], 0)
    sources = [(index, 0) for index in range(2)]
    return right_products(lefts, [inner, far], sources, order, 6 * LANES, near)


def general_plan(columns, counts, aggregate, matrix_blocks, payload, row_count, col_count):
    forward = [(i, i + 1) for i in range(row_count - 1)]
    backward = [(b, a) for a, b in forward]
    slab = lax.all_gather(payload, "cols", axis=0, tiled=True)
    pieces = [lax.ppermute(slab, "rows", forward), slab, lax.ppermute(slab, "rows", backward)]
    total = 3 * col_count
    order = lambda: [(block, None) for block in range(total)]
    lefts = left_sums(columns, counts, aggregate, payload, matrix_blocks, total, lambda: None)
    sources = [(slab, c * PAYLOAD) for slab in range(3) for c in range(col_count)]
    return right_products(lefts, pieces, sources, order, total * LANES, None)


def per_device(matrix_blocks, restrict, columns, counts, aggregate):
    col_count = lax.axis_size("cols")
    row_count = lax.axis_size("rows")
    payload = pack(aggregate, restrict)
    if col_count == 2 and row_count % 2 == 0:
        return paired_plan(columns, counts, aggregate, matrix_blocks, payload, row_count)
    return general_plan(
        columns, counts, aggregate, matrix_blocks, payload, row_count, col_count
    )


def solution(mesh):
    return jax.shard_map(
        per_device,
        mesh=mesh,
        in_specs=(
            P(("rows", "cols"), None, None),
            P(("rows", "cols"), None),
            P(("rows", "cols"), None),
            P(("rows", "cols")),
            P(("rows", "cols")),
        ),
        out_specs=P(("rows", "cols"), None, None),
        check_vma=False,
    )
```

```python
import functools

import jax
import jax.numpy as jnp
from jax import lax
from jax.experimental import pallas as pl
from jax.experimental.pallas import tpu as pltpu
from jax.sharding import PartitionSpec as P

BLK = 64
SLOTS = 27
ROWS_DEV = 32
AGG_DEV = 2

LANES = 2 * BLK
PAIRS = ROWS_DEV // 2
TAGS = PAIRS * BLK
PAYLOAD = TAGS + PAIRS
STEP = 4
BATCH = 4
CHUNK = 6
MIB = 1 << 20


def pack_kernel(aggregate_hbm, restrict_hbm, out_ref, restrict_ref, aggregate_ref, sems):
    rows = pltpu.make_async_copy(restrict_hbm, restrict_ref, sems.at[0])
    tags = pltpu.make_async_copy(aggregate_hbm, aggregate_ref, sems.at[1])
    rows.start()
    tags.start()
    tags.wait()
    row = lax.broadcasted_iota(jnp.int32, (PAIRS, LANES), 0)
    low = lax.broadcasted_iota(jnp.int32, (PAIRS, LANES), 1) < BLK
    owners = jnp.zeros((PAIRS, LANES), jnp.int32)
    for p in range(PAIRS):
        owner = jnp.where(low, aggregate_ref[p], aggregate_ref[p + PAIRS])
        owners = jnp.where(row == p, owner, owners)
    out_ref[TAGS:, :] = owners.astype(jnp.float32).astype(jnp.bfloat16)
    rows.wait()
    halves = []
    for t in range(BLK // 2):
        x = restrict_ref[:, t * LANES : (t + 1) * LANES].astype(jnp.float32)
        first, second = x[:PAIRS], x[PAIRS:]
        halves.append(jnp.where(low, first, pltpu.roll(second, BLK, 1)))
        halves.append(jnp.where(low, pltpu.roll(first, BLK, 1), second))
    blocks = jnp.stack(halves, axis=0).swapaxes(0, 1).reshape(TAGS, LANES)
    out_ref[:TAGS, :] = blocks.astype(jnp.bfloat16)


def pack(aggregate, restrict):
    hbm = pl.BlockSpec(memory_space=pltpu.HBM)
    return pl.pallas_call(
        pack_kernel,
        out_shape=jax.ShapeDtypeStruct((PAYLOAD, LANES), jnp.bfloat16),
        in_specs=[hbm, hbm],
        out_specs=pl.BlockSpec(memory_space=pltpu.VMEM),
        scratch_shapes=[
            pltpu.VMEM(restrict.shape, restrict.dtype),
            pltpu.SMEM(aggregate.shape, aggregate.dtype),
            pltpu.SemaphoreType.DMA((2,)),
        ],
        compiler_params=pltpu.CompilerParams(vmem_limit_bytes=8 * MIB),
        name="pack_payload",
    )(*(pltpu.with_memory_space_constraint(x, pltpu.HBM) for x in (aggregate, restrict)))


def left_kernel(
    order,
    columns_hbm,
    counts_hbm,
    aggregate_hbm,
    payload_ref,
    matrix_hbm,
    out_ref,
    matrix_ref,
    sums_ref,
    columns_ref,
    counts_ref,
    aggregate_ref,
    matrix_sems,
    sems,
):
    total = out_ref.shape[0]
    blocks = CHUNK if total % CHUNK == 0 else CHUNK // 2
    width = blocks * ROWS_DEV
    places = order()
    short = BLK // 2
    steps = PAIRS // STEP

    def rows_copy(step):
        cut = pl.ds(step * STEP, STEP)
        return pltpu.make_async_copy(
            matrix_hbm.at[:, cut], matrix_ref.at[:, cut], matrix_sems.at[step]
        )

    small = [
        pltpu.make_async_copy(columns_hbm, columns_ref, sems.at[0]),
        pltpu.make_async_copy(counts_hbm, counts_ref, sems.at[1]),
        pltpu.make_async_copy(aggregate_hbm, aggregate_ref, sems.at[2]),
    ]
    for copy in small:
        copy.start()
    for step in range(steps):
        rows_copy(step).start()
    low = lax.broadcasted_iota(jnp.int32, (BLK, LANES), 1) < BLK
    low_short = lax.broadcasted_iota(jnp.int32, (short, LANES), 1) < BLK

    def add_all(entries):
        entries = list(entries)
        for first in range(0, len(entries), BATCH):
            batch = entries[first : first + BATCH]
            values = [sums_ref[place] for place, _ in batch]
            for n, (place, tile) in enumerate(batch):
                for earlier in range(n):
                    values[n] = jnp.where(place == batch[earlier][0], values[earlier], values[n])
                values[n] = values[n] + tile
            for (place, _), value in zip(batch, values):
                sums_ref[place] = value

    def tiles_of(base, pair):
        both = payload_ref[pl.ds(pl.multiple_of(pair * BLK, BLK), BLK), :]
        zero = jnp.zeros_like(both)
        lhs = jnp.concatenate([jnp.where(low, both, zero), jnp.where(low, zero, both)], axis=0)
        rows = (pair, pair + PAIRS)
        count = [counts_ref[row] for row in rows]
        offset = [aggregate_ref[row] * width for row in rows]

        def place_of(r, k):
            local = columns_ref[rows[r], k]
            live = k < count[r]
            if total > blocks:
                local = local - base
                live = live & (local >= 0) & (local < width)
            return jnp.where(live, offset[r] + local, AGG_DEV * width)

        for first in range(0, SLOTS, 4):
            many = min(4, SLOTS - first)
            cut = slice(first * BLK, (first + many) * BLK)
            rhs = jnp.concatenate(
                [matrix_ref[0, pair, :, cut], matrix_ref[1, pair, :, cut]], axis=0
            )
            if many * BLK % LANES:
                rhs = jnp.concatenate([rhs, rhs[:, -BLK:]], axis=1)
            left = jnp.dot(lhs, rhs, preferred_element_type=jnp.float32).astype(jnp.bfloat16)
            for k in range(0, many, 2):
                for r in range(2):
                    lanes = slice(k * BLK, (k + 2) * BLK)
                    upper = left[r * BLK : r * BLK + short, lanes]
                    lower = left[r * BLK + short : (r + 1) * BLK, lanes]
                    one = jnp.where(low_short, upper, pltpu.roll(lower, BLK, 1))
                    yield place_of(r, first + k), one.astype(jnp.float32)
                    if k + 1 < many:
                        two = jnp.where(low_short, pltpu.roll(upper, BLK, 1), lower)
                        yield place_of(r, first + k + 1), two.astype(jnp.float32)

    def one_chunk(chunk, first_chunk):
        base = chunk * width
        sums_ref[...] = jnp.zeros_like(sums_ref)
        if first_chunk:
            for copy in small:
                copy.wait()

        def one_step(step, carry):
            if first_chunk:
                rows_copy(step).wait()
            add_all(
                entry for local in range(STEP) for entry in tiles_of(base, step * STEP + local)
            )
            return carry

        lax.fori_loop(0, steps, one_step, 0)
        for position in range(blocks):
            spot, live = places[position] if places is not None else (position, None)
            start = spot * ROWS_DEV
            for a in range(AGG_DEV):
                for p in range(PAIRS):
                    g = a * width + start + p
                    one, two = sums_ref[g], sums_ref[g + PAIRS]
                    if live is not None:
                        one, two = jnp.where(live, one, 0.0), jnp.where(live, two, 0.0)
                    one, two = one.astype(jnp.bfloat16), two.astype(jnp.bfloat16)
                    lanes = slice(p * LANES, (p + 1) * LANES)
                    out_ref[chunk * blocks + position, a * BLK : a * BLK + short, lanes] = (
                        jnp.where(low_short, one, pltpu.roll(two, BLK, 1))
                    )
                    out_ref[
                        chunk * blocks + position, a * BLK + short : (a + 1) * BLK, lanes
                    ] = jnp.where(low_short, pltpu.roll(one, BLK, 1), two)

    one_chunk(0, True)
    if total > blocks:

        def later(chunk, carry):
            one_chunk(chunk, False)
            return carry

        lax.fori_loop(1, total // blocks, later, 0)


def left_sums(columns, counts, aggregate, payload, matrix_blocks, total, order):
    blocks = CHUNK if total % CHUNK == 0 else CHUNK // 2
    matrix = matrix_blocks.reshape(2, PAIRS, BLK, SLOTS * BLK)
    hbm = pl.BlockSpec(memory_space=pltpu.HBM)
    vmem = pl.BlockSpec(memory_space=pltpu.VMEM)
    return pl.pallas_call(
        functools.partial(left_kernel, order),
        out_shape=jax.ShapeDtypeStruct((total, AGG_DEV * BLK, PAIRS * LANES), jnp.bfloat16),
        in_specs=[hbm, hbm, hbm, vmem, hbm],
        out_specs=vmem,
        scratch_shapes=[
            pltpu.VMEM(matrix.shape, matrix.dtype),
            pltpu.VMEM((AGG_DEV * blocks * ROWS_DEV + 1, BLK // 2, LANES), jnp.float32),
            pltpu.SMEM(columns.shape, columns.dtype),
            pltpu.SMEM(counts.shape, counts.dtype),
            pltpu.SMEM(aggregate.shape, aggregate.dtype),
            pltpu.SemaphoreType.DMA((PAIRS // STEP,)),
            pltpu.SemaphoreType.DMA((3,)),
        ],
        compiler_params=pltpu.CompilerParams(vmem_limit_bytes=20 * MIB),
        cost_estimate=pl.CostEstimate(
            flops=4 * ROWS_DEV * SLOTS * BLK**3, bytes_accessed=4 * MIB // 2, transcendentals=0
        ),
        name="left_sums",
    )(
        *(pltpu.with_memory_space_constraint(x, pltpu.HBM) for x in (columns, counts, aggregate)),
        payload,
        pltpu.with_memory_space_constraint(matrix, pltpu.HBM),
    )


def block_product(lefts, piece):
    tags = piece[TAGS:, :].astype(jnp.float32)
    masks = [(tags == j).astype(jnp.float32).astype(jnp.bfloat16) for j in range(AGG_DEV)]
    rhs = jnp.concatenate(
        [
            jnp.concatenate(
                [piece[p * BLK : (p + 1) * BLK, :] * masks[j][p : p + 1, :] for p in range(PAIRS)],
                axis=1,
            )
            for j in range(AGG_DEV)
        ],
        axis=0,
    )
    return lax.dot_general(
        lefts, rhs, (((1,), (1,)), ((), ())), preferred_element_type=jnp.float32
    )


def near_kernel(first, lefts_ref, *refs):
    out_ref = refs[-1]
    for position, piece in enumerate(refs[:-1]):
        total = block_product(lefts_ref[first + position], piece[...])
        for a in range(AGG_DEV):
            out_ref[position, a] = total[a * BLK : (a + 1) * BLK]


def near_products(lefts, pieces, first):
    many = len(pieces)
    vmem = pl.BlockSpec(memory_space=pltpu.VMEM)
    return pl.pallas_call(
        functools.partial(near_kernel, first),
        out_shape=jax.ShapeDtypeStruct((many, AGG_DEV, BLK, LANES), jnp.float32),
        in_specs=[vmem] * (1 + many),
        out_specs=vmem,
        compiler_params=pltpu.CompilerParams(vmem_limit_bytes=8 * MIB),
        cost_estimate=right_cost(many),
        name="near_products",
    )(lefts, *pieces)


def right_cost(many):
    return pl.CostEstimate(
        flops=2 * many * (AGG_DEV * BLK) ** 2 * PAIRS * LANES,
        bytes_accessed=many * MIB // 16,
        transcendentals=0,
    )


def right_kernel(sources, order, first, lefts_ref, *refs):
    out_hbm, columns_ref, sems = refs[-3:]
    copies = []

    def send(position, tile):
        place, _ = order()[position]
        place = place * LANES if isinstance(place, int) else pl.multiple_of(place * LANES, LANES)
        copy = pltpu.make_async_copy(
            tile, out_hbm.at[:, :, pl.ds(place, LANES)], sems.at[position]
        )
        copy.start()
        copies.append(copy)

    for position in range(first):
        send(position, refs[-4].at[position])
    for position, (index, start) in enumerate(sources):
        total = block_product(
            lefts_ref[first + position], refs[index][start : start + PAYLOAD, :]
        )
        for a in range(AGG_DEV):
            columns_ref[position, a] = total[a * BLK : (a + 1) * BLK]
        send(first + position, columns_ref.at[position])
    for copy in copies:
        copy.wait()


def right_products(lefts, pieces, sources, order, width, near):
    first = 0 if near is None else near.shape[0]
    many = len(sources)
    vmem = pl.BlockSpec(memory_space=pltpu.VMEM)
    return pl.pallas_call(
        functools.partial(right_kernel, sources, order, first),
        out_shape=jax.ShapeDtypeStruct((AGG_DEV, BLK, width), jnp.float32),
        in_specs=[vmem] * (1 + len(pieces) + (first > 0)),
        out_specs=pl.BlockSpec(memory_space=pltpu.HBM),
        scratch_shapes=[
            pltpu.VMEM((many, AGG_DEV, BLK, LANES), jnp.float32),
            pltpu.SemaphoreType.DMA((first + many,)),
        ],
        compiler_params=pltpu.CompilerParams(vmem_limit_bytes=8 * MIB),
        cost_estimate=right_cost(many),
        name="right_products",
    )(lefts, *pieces, *([near] if first else []))


def paired_plan(columns, counts, aggregate, matrix_blocks, payload, row_count):
    ring = [(i, (i + 1) % row_count) for i in range(row_count)]
    across = [(0, 1), (1, 0)]
    evens = [(i, i ^ 1) for i in range(row_count)]
    odds = [(i, i + 1) for i in range(1, row_count - 1, 2)]
    odds = odds + [(b, a) for a, b in odds] + [(0, 0), (row_count - 1, row_count - 1)]
    crossed = [(2 * a + c, 2 * b + 1 - c) for a, b in odds for c in range(2)]

    def order():
        c, row = lax.axis_index("cols"), lax.axis_index("rows")
        up = 1 - lax.rem(row, 2)
        low, high = row > 0, row < row_count - 1
        far = (up == 0) & high | (up == 1) & low
        return [
            (2 + c, None),
            (3 - c, None),
            (4 + c, high),
            (c, low),
            (4 * up + 1 - c, None),
            (4 - 4 * up + 1 - c, far),
        ]

    far = lax.ppermute(payload, ("rows", "cols"), crossed)
    beside = lax.ppermute(payload, "cols", across)
    below = lax.ppermute(payload, "rows", ring)
    above = lax.ppermute(payload, "rows", [(b, a) for a, b in ring])
    lefts = left_sums(columns, counts, aggregate, payload, matrix_blocks, 6, order)
    lefts, beside, above = lax.optimization_barrier((lefts, beside, above))
    inner = lax.ppermute(beside, "rows", evens)
    near = near_products(lefts, [payload, beside, above, below], 0)
    sources = [(index, 0) for index in range(2)]
    return right_products(lefts, [inner, far], sources, order, 6 * LANES, near)


def general_plan(columns, counts, aggregate, matrix_blocks, payload, row_count, col_count):
    forward = [(i, i + 1) for i in range(row_count - 1)]
    backward = [(b, a) for a, b in forward]
    slab = lax.all_gather(payload, "cols", axis=0, tiled=True)
    pieces = [lax.ppermute(slab, "rows", forward), slab, lax.ppermute(slab, "rows", backward)]
    total = 3 * col_count
    order = lambda: [(block, None) for block in range(total)]
    lefts = left_sums(columns, counts, aggregate, payload, matrix_blocks, total, lambda: None)
    sources = [(slab, c * PAYLOAD) for slab in range(3) for c in range(col_count)]
    return right_products(lefts, pieces, sources, order, total * LANES, None)


def per_device(matrix_blocks, restrict, columns, counts, aggregate):
    col_count = lax.axis_size("cols")
    row_count = lax.axis_size("rows")
    payload = pack(aggregate, restrict)
    if col_count == 2 and row_count % 2 == 0:
        return paired_plan(columns, counts, aggregate, matrix_blocks, payload, row_count)
    return general_plan(
        columns, counts, aggregate, matrix_blocks, payload, row_count, col_count
    )


def solution(mesh):
    return jax.shard_map(
        per_device,
        mesh=mesh,
        in_specs=(
            P(("rows", "cols"), None, None),
            P(("rows", "cols"), None),
            P(("rows", "cols"), None),
            P(("rows", "cols")),
            P(("rows", "cols")),
        ),
        out_specs=P(("rows", "cols"), None, None),
        check_vma=False,
    )
```

```python
import functools

import jax
import jax.numpy as jnp
from jax import lax
from jax.experimental import pallas as pl
from jax.experimental.pallas import tpu as pltpu
from jax.sharding import PartitionSpec as P

BLK = 64
SLOTS = 27
ROWS_DEV = 32
AGG_DEV = 2

LANES = 2 * BLK
PAIRS = ROWS_DEV // 2
TAGS = PAIRS * BLK
PAYLOAD = TAGS + PAIRS
STEP = 4
BATCH = 4
CHUNK = 6
MIB = 1 << 20


def pack_kernel(aggregate_hbm, restrict_hbm, out_ref, restrict_ref, aggregate_ref, sems):
    rows = pltpu.make_async_copy(restrict_hbm, restrict_ref, sems.at[0])
    tags = pltpu.make_async_copy(aggregate_hbm, aggregate_ref, sems.at[1])
    rows.start()
    tags.start()
    tags.wait()
    row = lax.broadcasted_iota(jnp.int32, (PAIRS, LANES), 0)
    low = lax.broadcasted_iota(jnp.int32, (PAIRS, LANES), 1) < BLK
    owners = jnp.zeros((PAIRS, LANES), jnp.int32)
    for p in range(PAIRS):
        owner = jnp.where(low, aggregate_ref[p], aggregate_ref[p + PAIRS])
        owners = jnp.where(row == p, owner, owners)
    out_ref[TAGS:, :] = owners.astype(jnp.float32).astype(jnp.bfloat16)
    rows.wait()
    halves = []
    for t in range(BLK // 2):
        x = restrict_ref[:, t * LANES : (t + 1) * LANES].astype(jnp.float32)
        first, second = x[:PAIRS], x[PAIRS:]
        halves.append(jnp.where(low, first, pltpu.roll(second, BLK, 1)))
        halves.append(jnp.where(low, pltpu.roll(first, BLK, 1), second))
    blocks = jnp.stack(halves, axis=0).swapaxes(0, 1).reshape(TAGS, LANES)
    out_ref[:TAGS, :] = blocks.astype(jnp.bfloat16)


def pack(aggregate, restrict):
    hbm = pl.BlockSpec(memory_space=pltpu.HBM)
    return pl.pallas_call(
        pack_kernel,
        out_shape=jax.ShapeDtypeStruct((PAYLOAD, LANES), jnp.bfloat16),
        in_specs=[hbm, hbm],
        out_specs=pl.BlockSpec(memory_space=pltpu.VMEM),
        scratch_shapes=[
            pltpu.VMEM(restrict.shape, restrict.dtype),
            pltpu.SMEM(aggregate.shape, aggregate.dtype),
            pltpu.SemaphoreType.DMA((2,)),
        ],
        compiler_params=pltpu.CompilerParams(vmem_limit_bytes=8 * MIB),
        name="pack_payload",
    )(*(pltpu.with_memory_space_constraint(x, pltpu.HBM) for x in (aggregate, restrict)))


def left_kernel(
    order,
    columns_hbm,
    counts_hbm,
    aggregate_hbm,
    payload_ref,
    matrix_hbm,
    out_ref,
    matrix_ref,
    sums_ref,
    columns_ref,
    counts_ref,
    aggregate_ref,
    matrix_sems,
    sems,
):
    total = out_ref.shape[0]
    blocks = CHUNK if total % CHUNK == 0 else CHUNK // 2
    width = blocks * ROWS_DEV
    places = order()
    short = BLK // 2
    steps = PAIRS // STEP

    def rows_copy(step):
        cut = pl.ds(step * STEP, STEP)
        return pltpu.make_async_copy(
            matrix_hbm.at[:, cut], matrix_ref.at[:, cut], matrix_sems.at[step]
        )

    small = [
        pltpu.make_async_copy(columns_hbm, columns_ref, sems.at[0]),
        pltpu.make_async_copy(counts_hbm, counts_ref, sems.at[1]),
        pltpu.make_async_copy(aggregate_hbm, aggregate_ref, sems.at[2]),
    ]
    for copy in small:
        copy.start()
    for step in range(steps):
        rows_copy(step).start()
    low = lax.broadcasted_iota(jnp.int32, (BLK, LANES), 1) < BLK
    low_short = lax.broadcasted_iota(jnp.int32, (short, LANES), 1) < BLK

    def add_all(entries):
        entries = list(entries)
        for first in range(0, len(entries), BATCH):
            batch = entries[first : first + BATCH]
            values = [sums_ref[place] for place, _ in batch]
            for n, (place, tile) in enumerate(batch):
                for earlier in range(n):
                    values[n] = jnp.where(place == batch[earlier][0], values[earlier], values[n])
                values[n] = values[n] + tile
            for (place, _), value in zip(batch, values):
                sums_ref[place] = value

    def tiles_of(base, pair):
        both = payload_ref[pl.ds(pl.multiple_of(pair * BLK, BLK), BLK), :]
        zero = jnp.zeros_like(both)
        lhs = jnp.concatenate([jnp.where(low, both, zero), jnp.where(low, zero, both)], axis=0)
        rows = (pair, pair + PAIRS)
        count = [counts_ref[row] for row in rows]
        offset = [aggregate_ref[row] * width for row in rows]

        def place_of(r, k):
            local = columns_ref[rows[r], k]
            live = k < count[r]
            if total > blocks:
                local = local - base
                live = live & (local >= 0) & (local < width)
            return jnp.where(live, offset[r] + local, AGG_DEV * width)

        for first in range(0, SLOTS, 4):
            many = min(4, SLOTS - first)
            cut = slice(first * BLK, (first + many) * BLK)
            rhs = jnp.concatenate(
                [matrix_ref[0, pair, :, cut], matrix_ref[1, pair, :, cut]], axis=0
            )
            if many * BLK % LANES:
                rhs = jnp.concatenate([rhs, rhs[:, -BLK:]], axis=1)
            left = jnp.dot(lhs, rhs, preferred_element_type=jnp.float32).astype(jnp.bfloat16)
            for k in range(0, many, 2):
                for r in range(2):
                    lanes = slice(k * BLK, (k + 2) * BLK)
                    upper = left[r * BLK : r * BLK + short, lanes]
                    lower = left[r * BLK + short : (r + 1) * BLK, lanes]
                    one = jnp.where(low_short, upper, pltpu.roll(lower, BLK, 1))
                    yield place_of(r, first + k), one.astype(jnp.float32)
                    if k + 1 < many:
                        two = jnp.where(low_short, pltpu.roll(upper, BLK, 1), lower)
                        yield place_of(r, first + k + 1), two.astype(jnp.float32)

    def one_chunk(chunk, first_chunk):
        base = chunk * width
        sums_ref[...] = jnp.zeros_like(sums_ref)
        if first_chunk:
            for copy in small:
                copy.wait()

        def one_step(step, carry):
            if first_chunk:
                rows_copy(step).wait()
            add_all(
                entry for local in range(STEP) for entry in tiles_of(base, step * STEP + local)
            )
            return carry

        lax.fori_loop(0, steps, one_step, 0)
        for position in range(blocks):
            spot, live = places[position] if places is not None else (position, None)
            start = spot * ROWS_DEV
            for a in range(AGG_DEV):
                for p in range(PAIRS):
                    g = a * width + start + p
                    one, two = sums_ref[g], sums_ref[g + PAIRS]
                    if live is not None:
                        one, two = jnp.where(live, one, 0.0), jnp.where(live, two, 0.0)
                    one, two = one.astype(jnp.bfloat16), two.astype(jnp.bfloat16)
                    lanes = slice(p * LANES, (p + 1) * LANES)
                    out_ref[chunk * blocks + position, a * BLK : a * BLK + short, lanes] = (
                        jnp.where(low_short, one, pltpu.roll(two, BLK, 1))
                    )
                    out_ref[
                        chunk * blocks + position, a * BLK + short : (a + 1) * BLK, lanes
                    ] = jnp.where(low_short, pltpu.roll(one, BLK, 1), two)

    one_chunk(0, True)
    if total > blocks:

        def later(chunk, carry):
            one_chunk(chunk, False)
            return carry

        lax.fori_loop(1, total // blocks, later, 0)


def left_sums(columns, counts, aggregate, payload, matrix_blocks, total, order):
    blocks = CHUNK if total % CHUNK == 0 else CHUNK // 2
    matrix = matrix_blocks.reshape(2, PAIRS, BLK, SLOTS * BLK)
    hbm = pl.BlockSpec(memory_space=pltpu.HBM)
    vmem = pl.BlockSpec(memory_space=pltpu.VMEM)
    return pl.pallas_call(
        functools.partial(left_kernel, order),
        out_shape=jax.ShapeDtypeStruct((total, AGG_DEV * BLK, PAIRS * LANES), jnp.bfloat16),
        in_specs=[hbm, hbm, hbm, vmem, hbm],
        out_specs=vmem,
        scratch_shapes=[
            pltpu.VMEM(matrix.shape, matrix.dtype),
            pltpu.VMEM((AGG_DEV * blocks * ROWS_DEV + 1, BLK // 2, LANES), jnp.float32),
            pltpu.SMEM(columns.shape, columns.dtype),
            pltpu.SMEM(counts.shape, counts.dtype),
            pltpu.SMEM(aggregate.shape, aggregate.dtype),
            pltpu.SemaphoreType.DMA((PAIRS // STEP,)),
            pltpu.SemaphoreType.DMA((3,)),
        ],
        compiler_params=pltpu.CompilerParams(vmem_limit_bytes=20 * MIB),
        cost_estimate=pl.CostEstimate(
            flops=4 * ROWS_DEV * SLOTS * BLK**3, bytes_accessed=4 * MIB // 2, transcendentals=0
        ),
        name="left_sums",
    )(
        *(pltpu.with_memory_space_constraint(x, pltpu.HBM) for x in (columns, counts, aggregate)),
        payload,
        pltpu.with_memory_space_constraint(matrix, pltpu.HBM),
    )


def block_product(lefts, piece):
    tags = piece[TAGS:, :].astype(jnp.float32)
    masks = [(tags == j).astype(jnp.float32).astype(jnp.bfloat16) for j in range(AGG_DEV)]
    rhs = jnp.concatenate(
        [
            jnp.concatenate(
                [piece[p * BLK : (p + 1) * BLK, :] * masks[j][p : p + 1, :] for p in range(PAIRS)],
                axis=1,
            )
            for j in range(AGG_DEV)
        ],
        axis=0,
    )
    return lax.dot_general(
        lefts, rhs, (((1,), (1,)), ((), ())), preferred_element_type=jnp.float32
    )


def near_kernel(first, lefts_ref, *refs):
    out_ref = refs[-1]
    for position, piece in enumerate(refs[:-1]):
        total = block_product(lefts_ref[first + position], piece[...])
        for a in range(AGG_DEV):
            out_ref[position, a] = total[a * BLK : (a + 1) * BLK]


def near_products(lefts, pieces, first):
    many = len(pieces)
    vmem = pl.BlockSpec(memory_space=pltpu.VMEM)
    return pl.pallas_call(
        functools.partial(near_kernel, first),
        out_shape=jax.ShapeDtypeStruct((many, AGG_DEV, BLK, LANES), jnp.float32),
        in_specs=[vmem] * (1 + many),
        out_specs=vmem,
        compiler_params=pltpu.CompilerParams(vmem_limit_bytes=8 * MIB),
        cost_estimate=right_cost(many),
        name="near_products",
    )(lefts, *pieces)


def right_cost(many):
    return pl.CostEstimate(
        flops=2 * many * (AGG_DEV * BLK) ** 2 * PAIRS * LANES,
        bytes_accessed=many * MIB // 16,
        transcendentals=0,
    )


def right_kernel(sources, order, first, lefts_ref, *refs):
    out_hbm, columns_ref, sems = refs[-3:]
    copies = []

    def send(position, tile):
        place, _ = order()[position]
        place = place * LANES if isinstance(place, int) else pl.multiple_of(place * LANES, LANES)
        copy = pltpu.make_async_copy(
            tile, out_hbm.at[:, :, pl.ds(place, LANES)], sems.at[position]
        )
        copy.start()
        copies.append(copy)

    for position in range(first):
        send(position, refs[-4].at[position])
    for position, (index, start) in enumerate(sources):
        total = block_product(
            lefts_ref[first + position], refs[index][start : start + PAYLOAD, :]
        )
        for a in range(AGG_DEV):
            columns_ref[position, a] = total[a * BLK : (a + 1) * BLK]
        send(first + position, columns_ref.at[position])
    for copy in copies:
        copy.wait()


def right_products(lefts, pieces, sources, order, width, near):
    first = 0 if near is None else near.shape[0]
    many = len(sources)
    vmem = pl.BlockSpec(memory_space=pltpu.VMEM)
    return pl.pallas_call(
        functools.partial(right_kernel, sources, order, first),
        out_shape=jax.ShapeDtypeStruct((AGG_DEV, BLK, width), jnp.float32),
        in_specs=[vmem] * (1 + len(pieces) + (first > 0)),
        out_specs=pl.BlockSpec(memory_space=pltpu.HBM),
        scratch_shapes=[
            pltpu.VMEM((many, AGG_DEV, BLK, LANES), jnp.float32),
            pltpu.SemaphoreType.DMA((first + many,)),
        ],
        compiler_params=pltpu.CompilerParams(vmem_limit_bytes=8 * MIB),
        cost_estimate=right_cost(many),
        name="right_products",
    )(lefts, *pieces, *([near] if first else []))


def paired_plan(columns, counts, aggregate, matrix_blocks, payload, row_count):
    ring = [(i, (i + 1) % row_count) for i in range(row_count)]
    across = [(0, 1), (1, 0)]
    evens = [(i, i ^ 1) for i in range(row_count)]
    odds = [(i, i + 1) for i in range(1, row_count - 1, 2)]
    odds = odds + [(b, a) for a, b in odds] + [(0, 0), (row_count - 1, row_count - 1)]
    crossed = [(2 * a + c, 2 * b + 1 - c) for a, b in odds for c in range(2)]

    def order():
        c, row = lax.axis_index("cols"), lax.axis_index("rows")
        up = 1 - lax.rem(row, 2)
        low, high = row > 0, row < row_count - 1
        far = (up == 0) & high | (up == 1) & low
        return [
            (2 + c, None),
            (3 - c, None),
            (4 + c, high),
            (c, low),
            (4 - 4 * up + 1 - c, far),
            (4 * up + 1 - c, None),
        ]

    far = lax.ppermute(payload, ("rows", "cols"), crossed)
    beside = lax.ppermute(payload, "cols", across)
    below = lax.ppermute(payload, "rows", ring)
    above = lax.ppermute(payload, "rows", [(b, a) for a, b in ring])
    lefts = left_sums(columns, counts, aggregate, payload, matrix_blocks, 6, order)
    lefts, beside = lax.optimization_barrier((lefts, beside))
    inner = lax.ppermute(beside, "rows", evens)
    near = near_products(lefts, [payload, beside, above, below], 0)
    sources = [(index, 0) for index in range(2)]
    return right_products(lefts, [far, inner], sources, order, 6 * LANES, near)


def general_plan(columns, counts, aggregate, matrix_blocks, payload, row_count, col_count):
    forward = [(i, i + 1) for i in range(row_count - 1)]
    backward = [(b, a) for a, b in forward]
    slab = lax.all_gather(payload, "cols", axis=0, tiled=True)
    pieces = [lax.ppermute(slab, "rows", forward), slab, lax.ppermute(slab, "rows", backward)]
    total = 3 * col_count
    order = lambda: [(block, None) for block in range(total)]
    lefts = left_sums(columns, counts, aggregate, payload, matrix_blocks, total, lambda: None)
    sources = [(slab, c * PAYLOAD) for slab in range(3) for c in range(col_count)]
    return right_products(lefts, pieces, sources, order, total * LANES, None)


def per_device(matrix_blocks, restrict, columns, counts, aggregate):
    col_count = lax.axis_size("cols")
    row_count = lax.axis_size("rows")
    payload = pack(aggregate, restrict)
    if col_count == 2 and row_count % 2 == 0:
        return paired_plan(columns, counts, aggregate, matrix_blocks, payload, row_count)
    return general_plan(
        columns, counts, aggregate, matrix_blocks, payload, row_count, col_count
    )


def solution(mesh):
    return jax.shard_map(
        per_device,
        mesh=mesh,
        in_specs=(
            P(("rows", "cols"), None, None),
            P(("rows", "cols"), None),
            P(("rows", "cols"), None),
            P(("rows", "cols")),
            P(("rows", "cols")),
        ),
        out_specs=P(("rows", "cols"), None, None),
        check_vma=False,
    )
```
